256 devices in a mesh: segment: 2 (over z_hi), mp: 16 (over y, x), dp: 8 (over z_lo, core).
Axes of the slice: x: 4, y: 4, z: 8 (z_hi: 2, z_lo: 4; z = z_hi * 4 + z_lo), core: 2. Of those that a mesh axis runs over, the one named last changes fastest.
Arguments:
- hidden: bfloat16 [32768, 3584], P(('segment', 'mp', 'dp')), may hold values from -6 to 6
- chat_owner_index: int32 [8192], P(('segment', 'mp', 'dp')), may hold values from 0 to 15, as said below
- thinker_to_talker_weight: bfloat16 [3584, 896], P('dp'), may hold values from -0.09375 to 0.09375
- attention_norm_gain: bfloat16 [896], replicated, may hold values from 0.099609375 to 1.8984375
- talker_query_weight: bfloat16 [896, 768], replicated, may hold values from -0.1875 to 0.1875
- talker_key_weight: bfloat16 [896, 256], replicated, may hold values from -0.1875 to 0.1875
- talker_value_weight: bfloat16 [896, 256], replicated, may hold values from -0.1875 to 0.1875
- talker_key_value_cache: bfloat16 [16384, 2, 48, 256], P(('segment', 'mp', 'dp')), may hold values from -360 to 360
- cache_fill_length: int32 [16384], P(('segment', 'mp', 'dp')), may hold values from 1 to 48
- noisy_flow_rows: bfloat16 [32768, 1024], P(('segment', 'mp', 'dp')), may hold values from -6 to 6
- flow_expand_weight: bfloat16 [2048, 1792], P('mp'), may hold values from -0.125 to 0.125
- flow_reduce_weight: bfloat16 [2048, 1024], P('mp'), may hold values from -0.125 to 0.125
Outputs:
- flowed: bfloat16 [32768, 1024], P(('segment', 'mp', 'dp'))
The draws below stay inside these ranges and needn't reach their ends.
Inputs may be any that keep to these rules, and one draw needn't show every extreme that they name: `chat_owner_index`: every owner is among the 16 mp devices of the source's own segment and dp index; a device sends at most 4 conversations to one owner, and in each segment and dp group one owner receives exactly 4 from every device of the group.
All inputs are finite; a program needn't handle non-finite values.
Results may differ from the reference program's by a relative error of at most 0.012.
Values may be sent and summed in bfloat16 or wider, within the bound.
A program may use at most 128 MiB of HBM per device.

```python
import jax
import jax.numpy as jnp
from jax import lax

D = 3584
TALKER_WIDTH = 896
QUERY_HEAD_COUNT = 6
KEY_VALUE_HEADS = 2
HEAD_SIZE = 128
FLOW_WIDTH = 1024
FLOW_HIDDEN = 2048
DECODE_STEPS = 4
CHATS_PER_DEVICE = 32
TALKER_POSITIONS = 48
CAPC = 4
SLOTS_DEV = 64
CONVS = 8192
ROWS = 32768
TOTAL_SLOTS = 16384
N_SEGMENT = 2
N_MP = 16
N_DP = 8
DEVICES = 256


def shuffled_owner(subkey, owner_row):
    return owner_row[jax.random.permutation(subkey, owner_row.shape[0])]


def draw_chat_owner_index(key, part):
    key = jax.random.fold_in(key, 11)
    key_busy, key_offset, key_shuffle = jax.random.split(key, 3)
    busy = jax.random.randint(key_busy, (N_SEGMENT, N_DP), 0, N_MP)
    device_block = jnp.arange(DEVICES, dtype=jnp.int32)
    segment_index = device_block // (N_MP * N_DP)
    dp_index = device_block % N_DP
    busy_owner = busy[segment_index, dp_index]
    offsets = jax.random.randint(key_offset, (DEVICES,), 0, N_MP - 1)
    position = jnp.arange(CHATS_PER_DEVICE, dtype=jnp.int32)
    cyclic = (position[None, :] - CAPC + offsets[:, None]) % (N_MP - 1)
    others = (busy_owner[:, None] + 1 + cyclic) % N_MP
    owners = jnp.where(position[None, :] < CAPC, busy_owner[:, None], others)
    shuffle_keys = jax.random.split(key_shuffle, DEVICES)
    owners = jax.vmap(shuffled_owner)(shuffle_keys, owners)
    return owners.reshape(CONVS).astype(jnp.int32)


def draw_cache_fill_length(key, part):
    key = jax.random.fold_in(key, 23)
    key_length, key_chosen = jax.random.split(key)
    lengths = jax.random.randint(key_length, (DEVICES, SLOTS_DEV), 1, TALKER_POSITIONS + 1)
    chosen = jax.random.randint(key_chosen, (DEVICES, 1), 0, SLOTS_DEV)
    lengths = jnp.where(jnp.arange(SLOTS_DEV, dtype=jnp.int32)[None, :] == chosen, TALKER_POSITIONS, lengths)
    return lengths.reshape(TOTAL_SLOTS).astype(jnp.int32)


def draw_talker_key_value_cache(key, part):
    key = jax.random.fold_in(key, 37)
    cached_key_rows = jax.random.fold_in(key, 0)
    cache_entries = jnp.clip(jax.random.normal(cached_key_rows, (TOTAL_SLOTS, 2, TALKER_POSITIONS, KEY_VALUE_HEADS * HEAD_SIZE), jnp.float32), -6.0, 6.0)
    return cache_entries.astype(jnp.bfloat16)


def shard_levels(stream_key, shape, shards, least, largest):
    loudness = 1.0
    for dim, shards_of in shards:
        draws = jax.random.uniform(jax.random.fold_in(jax.random.fold_in(stream_key, 6), dim), (shards_of,), jnp.float32, least / len(shards), largest / len(shards))
        loudness = loudness * jnp.repeat(jnp.exp(draws), shape[dim] // shards_of).reshape((-1,) + (1,) * (len(shape) - 1 - dim))
    return loudness


def noise(rng, extent, width, bound, pieces=(), kind=jnp.bfloat16):
    entries = jax.random.normal(rng, extent, jnp.float32) * width
    if len(pieces) > 0:
        entries = shard_levels(rng, extent, pieces, -0.22, 0.18) * entries
    return jnp.clip(entries, min=-bound, max=bound).astype(kind)


def setup_inputs(seed: int = 0) -> dict:
    streams_of = jax.random.split(jax.random.key(seed), 13)
    hidden = noise(streams_of[0], (ROWS, D), 1.0, 6.0, ((0, 256),))
    chat_owner_index = draw_chat_owner_index(jax.random.fold_in(streams_of[12], 71), 0)
    thinker_to_talker_weight = noise(streams_of[2], (D, TALKER_WIDTH), D ** -0.5, 0.09375, ((0, 8),))
    attention_norm_gain = jnp.clip(1.0 + 0.18 * jax.random.normal(streams_of[3], (TALKER_WIDTH,), jnp.float32), 0.099609375, 1.8984375).astype(jnp.bfloat16)
    talker_query_weight = noise(streams_of[4], (TALKER_WIDTH, QUERY_HEAD_COUNT * HEAD_SIZE), TALKER_WIDTH ** -0.5, 0.1875)
    talker_key_weight = noise(streams_of[5], (TALKER_WIDTH, KEY_VALUE_HEADS * HEAD_SIZE), TALKER_WIDTH ** -0.5, 0.1875)
    talker_value_weight = noise(streams_of[6], (TALKER_WIDTH, KEY_VALUE_HEADS * HEAD_SIZE), TALKER_WIDTH ** -0.5, 0.1875)
    talker_key_value_cache = draw_talker_key_value_cache(jax.random.fold_in(streams_of[12], 71), 0)
    cache_fill_length = draw_cache_fill_length(jax.random.fold_in(streams_of[12], 71), 0)
    noisy_flow_rows = noise(streams_of[9], (ROWS, FLOW_WIDTH), 1.0, 6.0, ((0, 256),))
    flow_expand_weight = noise(streams_of[10], (FLOW_HIDDEN, FLOW_WIDTH + QUERY_HEAD_COUNT * HEAD_SIZE), (FLOW_WIDTH + QUERY_HEAD_COUNT * HEAD_SIZE) ** -0.5, 0.125, ((0, 16),))
    flow_reduce_weight = noise(streams_of[11], (FLOW_HIDDEN, FLOW_WIDTH), FLOW_HIDDEN ** -0.5, 0.125, ((0, 16),))
    return dict(hidden=hidden, chat_owner_index=chat_owner_index, thinker_to_talker_weight=thinker_to_talker_weight, attention_norm_gain=attention_norm_gain, talker_query_weight=talker_query_weight, talker_key_weight=talker_key_weight, talker_value_weight=talker_value_weight, talker_key_value_cache=talker_key_value_cache, cache_fill_length=cache_fill_length, noisy_flow_rows=noisy_flow_rows, flow_expand_weight=flow_expand_weight, flow_reduce_weight=flow_reduce_weight)


def rms_scale(values):
    return values * lax.rsqrt(lax.optimization_barrier(jnp.mean(values * values, axis=-1, keepdims=True)) + 1e-06)

def owner_ranks(owners):
    onehot = (owners[:, None] == jnp.arange(N_MP, dtype=jnp.int32)[None, :]).astype(jnp.int32)
    before = jnp.cumsum(onehot, axis=0) - onehot
    return lax.optimization_barrier(jnp.sum(before * onehot, axis=1)).astype(jnp.int32)

def attend(query_rows, new_key_rows, new_value_rows, cached, lengths):
    conv_count = query_rows.shape[0]
    step_count = query_rows.shape[1]
    kv_heads = new_key_rows.shape[2] // HEAD_SIZE
    groups = query_rows.shape[2] // (HEAD_SIZE * kv_heads)
    cache_span = cached.shape[2]
    query_heads = query_rows.reshape(conv_count, step_count, kv_heads, groups, HEAD_SIZE).astype(jnp.float32)
    key_fresh = new_key_rows.reshape(conv_count, step_count, kv_heads, HEAD_SIZE).astype(jnp.float32)
    value_fresh = new_value_rows.reshape(conv_count, step_count, kv_heads, HEAD_SIZE).astype(jnp.float32)
    key_cached = cached[:, 0].reshape(conv_count, cache_span, kv_heads, HEAD_SIZE).astype(jnp.float32)
    value_cached = cached[:, 1].reshape(conv_count, cache_span, kv_heads, HEAD_SIZE).astype(jnp.float32)
    factor = HEAD_SIZE ** (-0.5)
    score_cached = jnp.einsum('stkgd,sckd->stkgc', query_heads, key_cached) * factor
    score_fresh = jnp.einsum('stkgd,sukd->stkgu', query_heads, key_fresh) * factor
    cache_live = jnp.arange(cache_span, dtype=jnp.int32)[None, :] < lengths[:, None]
    causal = jnp.arange(step_count)[None, :] <= jnp.arange(step_count)[:, None]
    score_cached = jnp.where(cache_live[:, None, None, None, :], score_cached, -jnp.inf)
    score_fresh = jnp.where(causal[None, :, None, None, :], score_fresh, -jnp.inf)
    peak_score = jnp.maximum(lax.optimization_barrier(jnp.max(score_cached, axis=-1)), lax.optimization_barrier(jnp.max(score_fresh, axis=-1)))
    prob_cached = jnp.exp(score_cached - peak_score[..., None])
    prob_fresh = jnp.exp(score_fresh - peak_score[..., None])
    weight_sum = lax.optimization_barrier(jnp.sum(prob_cached, axis=-1)) + lax.optimization_barrier(jnp.sum(prob_fresh, axis=-1))
    weight_cached = (prob_cached / weight_sum[..., None]).astype(jnp.bfloat16)
    weight_fresh = (prob_fresh / weight_sum[..., None]).astype(jnp.bfloat16)
    attended = jnp.einsum('stkgc,sckd->stkgd', weight_cached.astype(jnp.float32), value_cached)
    attended = attended + jnp.einsum('stkgu,sukd->stkgd', weight_fresh.astype(jnp.float32), value_fresh)
    return attended.reshape(conv_count, step_count, kv_heads * groups * HEAD_SIZE).astype(jnp.bfloat16)

def reference(hidden, chat_owner_index, thinker_to_talker_weight, attention_norm_gain, talker_query_weight, talker_key_weight, talker_value_weight, talker_key_value_cache, cache_fill_length, noisy_flow_rows, flow_expand_weight, flow_reduce_weight):
    projected = jnp.dot(hidden, thinker_to_talker_weight, preferred_element_type=jnp.float32).astype(jnp.bfloat16)
    normed = (rms_scale(projected.astype(jnp.float32)) * attention_norm_gain.astype(jnp.float32)).astype(jnp.bfloat16)
    query_rows = jnp.dot(normed, talker_query_weight, preferred_element_type=jnp.float32).astype(jnp.bfloat16)
    new_key_rows = jnp.dot(normed, talker_key_weight, preferred_element_type=jnp.float32).astype(jnp.bfloat16)
    new_value_rows = jnp.dot(normed, talker_value_weight, preferred_element_type=jnp.float32).astype(jnp.bfloat16)
    owner_rank = jax.vmap(owner_ranks)(chat_owner_index.reshape(DEVICES, CHATS_PER_DEVICE)).reshape(CONVS)
    conv_index = jnp.arange(CONVS, dtype=jnp.int32)
    source = conv_index // CHATS_PER_DEVICE
    segment_index = source // (N_MP * N_DP)
    mp_index = source // N_DP % N_MP
    dp_index = source % N_DP
    slot_in_cache = (((segment_index * N_MP + chat_owner_index) * N_DP + dp_index) * SLOTS_DEV + mp_index * CAPC + owner_rank).astype(jnp.int32)

    def single_block(inputs):
        block_queries, block_keys, block_values, block_slot = inputs
        cached = jnp.take(talker_key_value_cache, block_slot, axis=0)
        lengths = jnp.take(cache_fill_length, block_slot, axis=0)
        return attend(block_queries, block_keys, block_values, cached, lengths)
    talker_output = lax.map(single_block, (query_rows.reshape(DEVICES, CHATS_PER_DEVICE, DECODE_STEPS, QUERY_HEAD_COUNT * HEAD_SIZE), new_key_rows.reshape(DEVICES, CHATS_PER_DEVICE, DECODE_STEPS, KEY_VALUE_HEADS * HEAD_SIZE), new_value_rows.reshape(DEVICES, CHATS_PER_DEVICE, DECODE_STEPS, KEY_VALUE_HEADS * HEAD_SIZE), slot_in_cache.reshape(DEVICES, CHATS_PER_DEVICE)))
    talker_output = talker_output.reshape(ROWS, QUERY_HEAD_COUNT * HEAD_SIZE)
    paired_device = jnp.roll(talker_output, ROWS // 2, axis=0)
    flow_input_rows = jnp.concatenate([noisy_flow_rows, paired_device], axis=1)
    widened_hidden = lax.dot_general(flow_input_rows, flow_expand_weight, (((1,), (1,)), ((), ())), preferred_element_type=jnp.float32)
    feedforward_hidden = jax.nn.gelu(widened_hidden).astype(jnp.bfloat16)
    flow_velocity = jnp.dot(feedforward_hidden, flow_reduce_weight, preferred_element_type=jnp.float32)
    return (noisy_flow_rows.astype(jnp.float32) + 0.5 * flow_velocity).astype(jnp.bfloat16)
```

```python
import jax
import jax.numpy as jnp
from jax import lax
from jax.experimental import pallas as pl
from jax.experimental.pallas import tpu as pltpu
from jax.sharding import PartitionSpec as P

MESH = pl.DeviceIdType.MESH
BF = jnp.bfloat16
F32 = jnp.float32
NEG = -1e30
HID = 2816
EXP = 1792


def dot(a, b):
    return jnp.dot(a, b, preferred_element_type=F32)


def dot_t(a, b):
    return lax.dot_general(a, b, (((1,), (1,)), ((), ())), preferred_element_type=F32)


def kernel(
    hid_ref, own_ref, w_ref, gain_ref, wq_ref, wk_ref, wv_ref, kv_ref, len_ref, noisy_ref, fe_ref, fr_ref,
    out_ref,
    hid, wbuf, wqkv, kbuf, vbuf, noisy, er, bias, perm, perm_t, pacc, packed, inb, qkv, outb, retb, mine, part, hpre, hact,
    lsem, t_send, t_recv, ts_send, f_send1, f_send2, f_fwd1, f_fwd2, f_recv, fs_send, fs_recv,
    a_send, a_recv, r_send, r_recv, x_send, x_recv,
):
    s = lax.axis_index("segment")
    m = lax.axis_index("mp")
    d = lax.axis_index("dp")
    zl, c = d // 2, d % 2
    z = s * 4 + zl
    y, x = m // 4, m % 4
    sib = (s, m, zl * 2 + (1 - c))

    def zdev(dz):
        zz = (z + dz + 8) % 8
        return (zz // 4, m, (zz % 4) * 2 + c)

    def xydev(dx, dy):
        return (s, ((y + dy + 4) % 4) * 4 + (x + dx + 4) % 4, d)

    def rcopy(src, dst, ss, rs, dev):
        return pltpu.make_async_remote_copy(
            src_ref=src, dst_ref=dst, send_sem=ss, recv_sem=rs, device_id=dev, device_id_type=MESH
        )

    local = []

    def load(src, dst):
        cp = pltpu.make_async_copy(src, dst, lsem.at[len(local)])
        cp.start()
        local.append(cp)
        return cp

    own_e = []
    for cc in range(2):
        for a in range(2):
            rows = pl.ds(cc * 64 + a * 32, 32)
            own_e.append(load(fe_ref.at[rows], er.at[m, cc, a, :, pl.ds(0, EXP)]))
            own_e.append(load(fr_ref.at[rows], er.at[m, cc, a, :, pl.ds(EXP, 1024)]))
    own_w = [load(w_ref.at[pl.ds(h * 224, 224)], wbuf.at[zl, c, h]) for h in range(2)]
    own_h = [load(hid_ref.at[:, pl.ds(i * 896, 896)], hid.at[i]) for i in range(4)]
    own_q = [
        load(wq_ref, wqkv.at[:, pl.ds(0, 768)]),
        load(wk_ref, wqkv.at[:, pl.ds(768, 256)]),
        load(wv_ref, wqkv.at[:, pl.ds(1024, 256)]),
    ]
    own_n = load(noisy_ref, noisy)
    own_kv = []
    for i in range(4):
        own_kv.append(load(kv_ref.at[:, i, 0], kbuf.at[:, pl.ds(i * 48, 48)]))
        own_kv.append(load(kv_ref.at[:, i, 1], vbuf.at[:, pl.ds(i * 48, 48)]))

    barrier = pltpu.get_barrier_semaphore()

    def greet(k, _):
        pl.semaphore_signal(barrier, inc=1, device_id=(s, (m + k) % 16, d), device_id_type=MESH)
        return 0

    for dev in (zdev(1), zdev(-1), sib, zdev(4)):
        pl.semaphore_signal(barrier, inc=1, device_id=dev, device_id_type=MESH)
    lax.fori_loop(1, 16, greet, 0)

    r0 = lax.broadcasted_iota(jnp.int32, (16, 208), 0)
    j0 = lax.broadcasted_iota(jnp.int32, (16, 208), 1)
    u0 = j0 - 192
    fresh_ok = (j0 >= 192) & (u0 // 4 == r0 // 4) & (u0 % 4 <= r0 % 4)
    slot0 = j0 // 48
    pos0 = j0 % 48
    same = (j0 < 192) & (slot0 == r0 // 4)

    def make_bias(g, _):
        ln = jnp.zeros((16, 208), jnp.int32)
        for i in range(4):
            ln = jnp.where(slot0 == i, len_ref[g * 4 + i], ln)
        ok = fresh_ok | (same & (pos0 < ln))
        bias[g] = jnp.where(ok, 0.0, NEG)
        return 0

    lax.fori_loop(0, 16, make_bias, 0)

    ri = lax.broadcasted_iota(jnp.int32, (128, 128), 0)
    ci = lax.broadcasted_iota(jnp.int32, (128, 128), 1)

    def owners(k, carry):
        a, b = carry
        o = own_ref[k]
        return jnp.where(ri // 4 == k, o, a), jnp.where(ci // 4 == k, o, b)

    zero = jnp.zeros((128, 128), jnp.int32)
    own_rows, own_cols = lax.fori_loop(0, 32, owners, (zero, zero))
    eq = own_rows == own_cols
    rank_row = jnp.sum(jnp.where(eq & (ri // 4 < ci // 4) & (ri % 4 == 0), 1.0, 0.0), axis=0, keepdims=True)
    rank_col = jnp.sum(jnp.where(eq & (ci // 4 < ri // 4) & (ci % 4 == 0), 1.0, 0.0), axis=1, keepdims=True)
    tgt_row = own_cols[0:1, :] * 16 + rank_row.astype(jnp.int32) * 4 + ci[0:1, :] % 4
    tgt_col = own_rows[:, 0:1] * 16 + rank_col.astype(jnp.int32) * 4 + ri[:, 0:1] % 4
    perm[...] = jnp.where(lax.broadcasted_iota(jnp.int32, (256, 128), 0) == tgt_row, 1.0, 0.0).astype(BF)
    perm_t[...] = jnp.where(lax.broadcasted_iota(jnp.int32, (128, 256), 1) == tgt_col, 1.0, 0.0).astype(BF)

    for cp in own_e:
        cp.wait()
    pl.semaphore_wait(barrier, 19)

    sends = []

    def go(cp):
        cp.start()
        sends.append(cp)

    def wcopy(zi, h, ss, dev, src=None):
        dst = wbuf.at[zi, c, h]
        return rcopy(dst if src is None else src, dst, ss, t_recv.at[zi, c, h], dev)

    for k in range(2):
        go(wcopy(zl, k, t_send.at[k], zdev(1), w_ref.at[pl.ds(k * 224, 224)]))
        go(wcopy(zl, 1 - k, t_send.at[2 + k], zdev(-1), w_ref.at[pl.ds((1 - k) * 224, 224)]))
    for k in range(2):
        go(wcopy(zl, k, ts_send.at[zl, k], sib, w_ref.at[pl.ds(k * 224, 224)]))

    def pid(a, i, j):
        return j * 4 + i if a == 0 else i * 4 + j

    def nb1(a, k):
        return xydev(k, 0) if a == 0 else xydev(0, k)

    def nb2(a, k):
        return xydev(0, k) if a == 0 else xydev(k, 0)

    def at(a):
        return (x, y) if a == 0 else (y, x)

    def full(p, a, ss, rs, dev):
        return rcopy(er.at[p, c, a], er.at[p, c, a], ss, rs, dev)

    def piece(p, a, k, ss, dev):
        ref = er.at[p, c, a, pl.ds(k * 16, 16)]
        return rcopy(ref, ref, ss, f_recv.at[p, a, k], dev)

    def got(p, a):
        full(p, a, f_send1.at[0, 0], f_recv.at[p, a, 0], sib).wait_recv()

    def got_piece(p, a, k):
        piece(p, a, k, f_send1.at[0, 0], sib).wait_recv()

    def share(p, a):
        cp = full(p, a, fs_send.at[p, a], fs_recv.at[p, a], sib)
        cp.start()

    def spread(a, i, j):
        p = pid(a, i, j)
        for k in range(2):
            full(p, a, f_send2.at[a, i, k], f_recv.at[p, a, 0], nb2(a, 1 - 2 * k)).start()

    for a in range(2):
        i, j = at(a)
        p = pid(a, i, j)
        for k in range(2):
            go(full(p, a, f_send1.at[a, k], f_recv.at[p, a, 0], nb1(a, 1 - 2 * k)))
    for a in range(2):
        spread(a, *at(a))
    for a in range(2):
        i, j = at(a)
        for k in range(2):
            i1 = (i + (3 if k == 0 else 1)) % 4
            p = pid(a, i1, j)
            got(p, a)
            go(piece(p, a, k, f_fwd1.at[a, k], nb1(a, 1 - 2 * k)))
            spread(a, i1, j)
            share(p, a)
    for a in range(2):
        i, j = at(a)
        i2 = (i + 2) % 4
        p = pid(a, i2, j)
        got_piece(p, a, 0)
        got_piece(p, a, 1)
        spread(a, i2, j)
        share(p, a)

    for cp in own_h + own_w:
        cp.wait()
    zm, zp, z2 = (zl + 3) % 4, (zl + 1) % 4, (zl + 2) % 4

    def wgot(zi, cc, h):
        dst = wbuf.at[zi, cc, h]
        rcopy(dst, dst, t_send.at[0], t_recv.at[zi, cc, h], sib).wait_recv()

    def wshare(zi, h):
        dst = wbuf.at[zi, c, h]
        rcopy(dst, dst, ts_send.at[zi, h], t_recv.at[zi, c, h], sib).start()

    def second(t, _):
        for a in range(2):
            i, j = at(a)
            it = (i + t) % 4
            for k in range(2):
                p = pid(a, it, (j + (3 if k == 0 else 1)) % 4)
                got(p, a)
                piece(p, a, k, f_fwd2.at[a, it, k], nb2(a, 1 - 2 * k)).start()
                share(p, a)
        return 0

    lax.fori_loop(0, 2, second, 0)
    for h in range(2):
        wgot(zl, 1 - c, h)
    pacc[...] = dot(hid[zl], wbuf[zl].reshape(896, 896))
    wgot(zm, c, 0)
    go(wcopy(zm, 0, t_send.at[4], zdev(1)))
    wgot(zp, c, 1)
    go(wcopy(zp, 1, t_send.at[5], zdev(-1)))
    wshare(zm, 0)
    wshare(zp, 1)
    lax.fori_loop(2, 4, second, 0)
    wgot(zm, c, 1)
    wshare(zm, 1)
    wgot(zp, c, 0)
    wshare(zp, 0)
    for zi in (zm, zp):
        for h in range(2):
            wgot(zi, 1 - c, h)
        pacc[...] += dot(hid[zi], wbuf[zi].reshape(896, 896))
    for h in range(2):
        wgot(z2, c, h)
        wshare(z2, h)
    for h in range(2):
        wgot(z2, 1 - c, h)
    projected = (pacc[...] + dot(hid[z2], wbuf[z2].reshape(896, 896))).astype(BF).astype(F32)
    scale = lax.rsqrt(jnp.mean(projected * projected, axis=-1, keepdims=True) + 1e-06)
    normed = (projected * scale * gain_ref[...].astype(F32)).astype(BF)
    packed[...] = dot(perm[...], normed).astype(BF).reshape(16, 16, 896)

    def post(k, _):
        o = (m + k) % 16
        rcopy(packed.at[o], inb.at[m], a_send.at[o], a_recv.at[m], (s, o, d)).start()
        return 0

    lax.fori_loop(1, 16, post, 0)
    inb[m] = packed[m]

    def third(t, _):
        for a in range(2):
            i, j = at(a)
            p = pid(a, (i + t) % 4, (j + 2) % 4)
            got_piece(p, a, 0)
            got_piece(p, a, 1)
            share(p, a)
        return 0

    lax.fori_loop(0, 4, third, 0)
    for cp in own_q + own_kv + [own_n]:
        cp.wait()

    def arrive(k, _):
        o = (m + k) % 16
        rcopy(packed.at[o], inb.at[o], a_send.at[o], a_recv.at[o], (s, o, d)).wait()
        return 0

    lax.fori_loop(1, 16, arrive, 0)
    qkv[...] = dot(inb[...].reshape(256, 896), wqkv[...]).astype(BF).reshape(16, 16, 1280)
    kbuf[:, 192:208, :] = qkv[:, :, 768:1024]
    vbuf[:, 192:208, :] = qkv[:, :, 1024:1280]

    factor = 128 ** (-0.5)

    def attend(q4, _):
        for gg in range(4):
            g = q4 * 4 + gg
            for h in range(2):
                q = jnp.concatenate(
                    [qkv[g, :, (h * 3 + e) * 128 : (h * 3 + e + 1) * 128] for e in range(3)], axis=0
                )
                sc = dot_t(q, kbuf[g, :, h * 128 : (h + 1) * 128]) * factor
                sc = sc.reshape(3, 16, 208) + bias[g][None]
                pk = jnp.max(sc, axis=-1, keepdims=True)
                pr = jnp.exp(sc - pk)
                wt = (pr / jnp.sum(pr, axis=-1, keepdims=True)).astype(BF)
                o = dot(wt.reshape(48, 208), vbuf[g, :, h * 128 : (h + 1) * 128]).astype(BF)
                for e in range(3):
                    outb[g, :, (h * 3 + e) * 128 : (h * 3 + e + 1) * 128] = o[e * 16 : (e + 1) * 16]
        for gg in range(4):
            g = q4 * 4 + gg

            @pl.when(g != m)
            def _():
                rcopy(outb.at[g], retb.at[m], r_send.at[g], r_recv.at[m], (s, g, d)).start()

        return 0

    lax.fori_loop(0, 4, attend, 0)
    retb[m] = outb[m]

    def back(k, _):
        o = (m + k) % 16
        rcopy(outb.at[o], retb.at[o], r_send.at[o], r_recv.at[o], (s, o, d)).wait()
        return 0

    lax.fori_loop(1, 16, back, 0)
    mine[...] = dot(perm_t[...], retb[...].reshape(256, 768)).astype(BF)
    swap = rcopy(mine, part, x_send.at[0], x_recv.at[0], zdev(4))
    swap.start()

    def shared(t, _):
        p = (m + t) % 16
        for a in range(2):
            dst = er.at[p, 1 - c, a]
            rcopy(dst, dst, fs_send.at[p, a], fs_recv.at[p, a], sib).wait_recv()
            full(p, a, fs_send.at[p, a], fs_recv.at[p, a], sib).wait_send()
        return 0

    lax.fori_loop(1, 16, shared, 0)

    def early(t, _):
        e = er[pl.ds(t * 2, 2), :, :, :, 0:1024].reshape(256, 1024)
        hpre[t] = dot_t(noisy[...], e)
        return 0

    lax.fori_loop(0, 8, early, 0)
    swap.wait()

    def late(t, _):
        e = er[pl.ds(t * 2, 2), :, :, :, 1024:EXP].reshape(256, 768)
        hact[t] = jax.nn.gelu(hpre[t] + dot_t(part[...], e)).astype(BF)
        return 0

    lax.fori_loop(0, 8, late, 0)
    h = jnp.concatenate([hact[t] for t in range(8)], axis=1)
    for n in range(4):
        cols = slice(n * 256, (n + 1) * 256)
        r = er[:, :, :, :, EXP + n * 256 : EXP + (n + 1) * 256].reshape(2048, 256)
        out_ref[:, cols] = (noisy[:, cols].astype(F32) + 0.5 * dot(h, r)).astype(BF)

    for cp in sends:
        cp.wait_send()
    for zi in (zm, zp, z2):
        for hh in range(2):
            dst = wbuf.at[zi, c, hh]
            rcopy(dst, dst, ts_send.at[zi, hh], t_recv.at[zi, c, hh], sib).wait_send()

    def sent(i, _):
        for a in range(2):
            p = pid(a, i, at(a)[1])
            for k in range(2):
                full(p, a, f_send2.at[a, i, k], f_recv.at[p, a, 0], sib).wait_send()
                piece(p, a, k, f_fwd2.at[a, i, k], sib).wait_send()
        return 0

    lax.fori_loop(0, 4, sent, 0)


def shards(hidden, owner, w, gain, wq, wk, wv, cache, fill, noisy, fe, fr):
    any_ = pl.BlockSpec(memory_space=pl.ANY)
    smem = pl.BlockSpec(memory_space=pltpu.SMEM)
    vmem = pl.BlockSpec(memory_space=pltpu.VMEM)
    dma = pltpu.SemaphoreType.DMA
    return pl.pallas_call(
        kernel,
        out_shape=jax.ShapeDtypeStruct((128, 1024), BF),
        in_specs=[any_, smem, any_, vmem, any_, any_, any_, any_, smem, any_, any_, any_],
        out_specs=vmem,
        scratch_shapes=[
            pltpu.VMEM((4, 128, 896), BF),
            pltpu.VMEM((4, 2, 2, 224, 896), BF),
            pltpu.VMEM((896, 1280), BF),
            pltpu.VMEM((16, 208, 256), BF),
            pltpu.VMEM((16, 208, 256), BF),
            pltpu.VMEM((128, 1024), BF),
            pltpu.VMEM((16, 2, 2, 32, HID), BF),
            pltpu.VMEM((16, 16, 208), F32),
            pltpu.VMEM((256, 128), BF),
            pltpu.VMEM((128, 256), BF),
            pltpu.VMEM((128, 896), F32),
            pltpu.VMEM((16, 16, 896), BF),
            pltpu.VMEM((16, 16, 896), BF),
            pltpu.VMEM((16, 16, 1280), BF),
            pltpu.VMEM((16, 16, 768), BF),
            pltpu.VMEM((16, 16, 768), BF),
            pltpu.VMEM((128, 768), BF),
            pltpu.VMEM((128, 768), BF),
            pltpu.VMEM((8, 128, 256), F32),
            pltpu.VMEM((8, 128, 256), BF),
            dma((32,)),
            dma((6,)),
            dma((4, 2, 2)),
            dma((4, 2)),
            dma((2, 2)),
            dma((2, 4, 2)),
            dma((2, 2)),
            dma((2, 4, 2)),
            dma((16, 2, 2)),
            dma((16, 2)),
            dma((16, 2)),
            dma((16,)),
            dma((16,)),
            dma((16,)),
            dma((16,)),
            dma((1,)),
            dma((1,)),
        ],
        compiler_params=pltpu.CompilerParams(
            collective_id=0, has_side_effects=True, vmem_limit_bytes=50 * 2**20
        ),
        name="talker_flow",
    )(
        hidden, owner, w, gain.reshape(1, 896), wq, wk, wv, cache.reshape(16, 4, 2, 48, 256), fill, noisy, fe, fr,
    )


def solution(mesh):
    placed = (
        P(("segment", "mp", "dp"), None),
        P(("segment", "mp", "dp")),
        P("dp", None),
        P(),
        P(),
        P(),
        P(),
        P(("segment", "mp", "dp"), None, None, None),
        P(("segment", "mp", "dp")),
        P(("segment", "mp", "dp"), None),
        P("mp", None),
        P("mp", None),
    )
    return jax.shard_map(
        shards,
        mesh=mesh,
        in_specs=placed,
        out_specs=P(("segment", "mp", "dp"), None),
        check_vma=False,
    )
```

```python
import jax
import jax.numpy as jnp
from jax import lax
from jax.experimental import pallas as pl
from jax.experimental.pallas import tpu as pltpu
from jax.sharding import PartitionSpec as P

MESH = pl.DeviceIdType.MESH
BF = jnp.bfloat16
F32 = jnp.float32
NEG = -1e30
HID = 2816
EXP = 1792


def dot(a, b):
    return jnp.dot(a, b, preferred_element_type=F32)


def dot_t(a, b):
    return lax.dot_general(a, b, (((1,), (1,)), ((), ())), preferred_element_type=F32)


def kernel(
    hid_ref, own_hbm, w_ref, gain_ref, wq_ref, wk_ref, wv_ref, kv_ref, len_hbm, noisy_ref, fe_ref, fr_ref,
    out_ref,
    own_ref, len_ref, hid, wbuf, wqkv, kbuf, vbuf, noisy, er, bias, perm, perm_t, pacc, packed, inb, qkv, outb, retb, mine, part, hpre, hact,
    lsem, t_send, t_recv, ts_send, f_send1, f_send2, f_fwd1, f_fwd2, f_recv, fs_send, fs_recv,
    a_send, a_recv, r_send, r_recv, x_send, x_recv,
):
    s = lax.axis_index("segment")
    m = lax.axis_index("mp")
    d = lax.axis_index("dp")
    zl, c = d // 2, d % 2
    z = s * 4 + zl
    y, x = m // 4, m % 4
    sib = (s, m, zl * 2 + (1 - c))

    def zdev(dz):
        zz = (z + dz + 8) % 8
        return (zz // 4, m, (zz % 4) * 2 + c)

    def xydev(dx, dy):
        return (s, ((y + dy + 4) % 4) * 4 + (x + dx + 4) % 4, d)

    def rcopy(src, dst, ss, rs, dev):
        return pltpu.make_async_remote_copy(
            src_ref=src, dst_ref=dst, send_sem=ss, recv_sem=rs, device_id=dev, device_id_type=MESH
        )

    barrier = pltpu.get_barrier_semaphore()

    def greet(k, _):
        pl.semaphore_signal(barrier, inc=1, device_id=(s, (m + k) % 16, d), device_id_type=MESH)
        return 0

    for dev in (zdev(1), zdev(-1), sib, zdev(4)):
        pl.semaphore_signal(barrier, inc=1, device_id=dev, device_id_type=MESH)
    lax.fori_loop(1, 16, greet, 0)

    local = []

    def load(src, dst):
        cp = pltpu.make_async_copy(src, dst, lsem.at[len(local)])
        cp.start()
        local.append(cp)
        return cp

    own_s = [load(own_hbm, own_ref), load(len_hbm, len_ref)]
    own_e = []
    for cc in range(2):
        for a in range(2):
            rows = pl.ds(cc * 64 + a * 32, 32)
            own_e.append(load(fe_ref.at[rows], er.at[m, cc, a, :, pl.ds(0, EXP)]))
            own_e.append(load(fr_ref.at[rows], er.at[m, cc, a, :, pl.ds(EXP, 1024)]))
    own_w = [load(w_ref.at[pl.ds(h * 224, 224)], wbuf.at[zl, c, h]) for h in range(2)]
    own_h = [load(hid_ref.at[:, pl.ds(i * 896, 896)], hid.at[i]) for i in range(4)]
    own_q = [
        load(wq_ref, wqkv.at[:, pl.ds(0, 768)]),
        load(wk_ref, wqkv.at[:, pl.ds(768, 256)]),
        load(wv_ref, wqkv.at[:, pl.ds(1024, 256)]),
    ]
    own_n = load(noisy_ref, noisy)
    own_kv = []
    for i in range(4):
        own_kv.append(load(kv_ref.at[:, i, 0], kbuf.at[:, pl.ds(i * 48, 48)]))
        own_kv.append(load(kv_ref.at[:, i, 1], vbuf.at[:, pl.ds(i * 48, 48)]))

    for cp in own_s:
        cp.wait()
    r0 = lax.broadcasted_iota(jnp.int32, (16, 208), 0)
    j0 = lax.broadcasted_iota(jnp.int32, (16, 208), 1)
    u0 = j0 - 192
    fresh_ok = (j0 >= 192) & (u0 // 4 == r0 // 4) & (u0 % 4 <= r0 % 4)
    slot0 = j0 // 48
    pos0 = j0 % 48
    same = (j0 < 192) & (slot0 == r0 // 4)

    def make_bias(g, _):
        ln = jnp.zeros((16, 208), jnp.int32)
        for i in range(4):
            ln = jnp.where(slot0 == i, len_ref[g * 4 + i], ln)
        ok = fresh_ok | (same & (pos0 < ln))
        bias[g] = jnp.where(ok, 0.0, NEG)
        return 0

    lax.fori_loop(0, 16, make_bias, 0)

    ri = lax.broadcasted_iota(jnp.int32, (128, 128), 0)
    ci = lax.broadcasted_iota(jnp.int32, (128, 128), 1)

    def owners(k, carry):
        a, b = carry
        o = own_ref[k]
        return jnp.where(ri // 4 == k, o, a), jnp.where(ci // 4 == k, o, b)

    zero = jnp.zeros((128, 128), jnp.int32)
    own_rows, own_cols = lax.fori_loop(0, 32, owners, (zero, zero))
    eq = own_rows == own_cols
    rank_row = jnp.sum(jnp.where(eq & (ri // 4 < ci // 4) & (ri % 4 == 0), 1.0, 0.0), axis=0, keepdims=True)
    rank_col = jnp.sum(jnp.where(eq & (ci // 4 < ri // 4) & (ci % 4 == 0), 1.0, 0.0), axis=1, keepdims=True)
    tgt_row = own_cols[0:1, :] * 16 + rank_row.astype(jnp.int32) * 4 + ci[0:1, :] % 4
    tgt_col = own_rows[:, 0:1] * 16 + rank_col.astype(jnp.int32) * 4 + ri[:, 0:1] % 4
    perm[...] = jnp.where(lax.broadcasted_iota(jnp.int32, (256, 128), 0) == tgt_row, 1.0, 0.0).astype(BF)
    perm_t[...] = jnp.where(lax.broadcasted_iota(jnp.int32, (128, 256), 1) == tgt_col, 1.0, 0.0).astype(BF)

    for cp in own_e:
        cp.wait()
    pl.semaphore_wait(barrier, 19)

    sends = []

    def go(cp):
        cp.start()
        sends.append(cp)

    def wcopy(zi, h, ss, dev, src=None):
        dst = wbuf.at[zi, c, h]
        return rcopy(dst if src is None else src, dst, ss, t_recv.at[zi, c, h], dev)

    for k in range(2):
        go(wcopy(zl, k, t_send.at[k], zdev(1), w_ref.at[pl.ds(k * 224, 224)]))
        go(wcopy(zl, 1 - k, t_send.at[2 + k], zdev(-1), w_ref.at[pl.ds((1 - k) * 224, 224)]))
    for k in range(2):
        go(wcopy(zl, k, ts_send.at[zl, k], sib, w_ref.at[pl.ds(k * 224, 224)]))

    def pid(a, i, j):
        return j * 4 + i if a == 0 else i * 4 + j

    def nb1(a, k):
        return xydev(k, 0) if a == 0 else xydev(0, k)

    def nb2(a, k):
        return xydev(0, k) if a == 0 else xydev(k, 0)

    def at(a):
        return (x, y) if a == 0 else (y, x)

    def full(p, a, ss, rs, dev):
        return rcopy(er.at[p, c, a], er.at[p, c, a], ss, rs, dev)

    def piece(p, a, k, ss, dev):
        ref = er.at[p, c, a, pl.ds(k * 16, 16)]
        return rcopy(ref, ref, ss, f_recv.at[p, a, k], dev)

    def got(p, a):
        full(p, a, f_send1.at[0, 0], f_recv.at[p, a, 0], sib).wait_recv()

    def got_piece(p, a, k):
        piece(p, a, k, f_send1.at[0, 0], sib).wait_recv()

    def share(p, a):
        cp = full(p, a, fs_send.at[p, a], fs_recv.at[p, a], sib)
        cp.start()

    def spread(a, i, j):
        p = pid(a, i, j)
        for k in range(2):
            full(p, a, f_send2.at[a, i, k], f_recv.at[p, a, 0], nb2(a, 1 - 2 * k)).start()

    for a in range(2):
        i, j = at(a)
        p = pid(a, i, j)
        for k in range(2):
            go(full(p, a, f_send1.at[a, k], f_recv.at[p, a, 0], nb1(a, 1 - 2 * k)))
    for a in range(2):
        spread(a, *at(a))
    for a in range(2):
        i, j = at(a)
        for k in range(2):
            i1 = (i + (3 if k == 0 else 1)) % 4
            p = pid(a, i1, j)
            got(p, a)
            go(piece(p, a, k, f_fwd1.at[a, k], nb1(a, 1 - 2 * k)))
            spread(a, i1, j)
            share(p, a)
    for a in range(2):
        i, j = at(a)
        i2 = (i + 2) % 4
        p = pid(a, i2, j)
        got_piece(p, a, 0)
        got_piece(p, a, 1)
        spread(a, i2, j)
        share(p, a)

    for cp in own_h + own_w:
        cp.wait()
    zm, zp, z2 = (zl + 3) % 4, (zl + 1) % 4, (zl + 2) % 4

    def wgot(zi, cc, h):
        dst = wbuf.at[zi, cc, h]
        rcopy(dst, dst, t_send.at[0], t_recv.at[zi, cc, h], sib).wait_recv()

    def wshare(zi, h):
        dst = wbuf.at[zi, c, h]
        rcopy(dst, dst, ts_send.at[zi, h], t_recv.at[zi, c, h], sib).start()

    def second(t, _):
        for a in range(2):
            i, j = at(a)
            it = (i + t) % 4
            for k in range(2):
                p = pid(a, it, (j + (3 if k == 0 else 1)) % 4)
                got(p, a)
                piece(p, a, k, f_fwd2.at[a, it, k], nb2(a, 1 - 2 * k)).start()
                share(p, a)
        return 0

    lax.fori_loop(0, 2, second, 0)
    for h in range(2):
        wgot(zl, 1 - c, h)
    pacc[...] = dot(hid[zl], wbuf[zl].reshape(896, 896))
    wgot(zm, c, 0)
    go(wcopy(zm, 0, t_send.at[4], zdev(1)))
    wgot(zp, c, 1)
    go(wcopy(zp, 1, t_send.at[5], zdev(-1)))
    wshare(zm, 0)
    wshare(zp, 1)
    lax.fori_loop(2, 4, second, 0)
    wgot(zm, c, 1)
    wshare(zm, 1)
    wgot(zp, c, 0)
    wshare(zp, 0)
    for zi in (zm, zp):
        for h in range(2):
            wgot(zi, 1 - c, h)
        pacc[...] += dot(hid[zi], wbuf[zi].reshape(896, 896))
    for h in range(2):
        wgot(z2, c, h)
        wshare(z2, h)
    for h in range(2):
        wgot(z2, 1 - c, h)
    projected = (pacc[...] + dot(hid[z2], wbuf[z2].reshape(896, 896))).astype(BF).astype(F32)
    scale = lax.rsqrt(jnp.mean(projected * projected, axis=-1, keepdims=True) + 1e-06)
    normed = (projected * scale * gain_ref[...].astype(F32).reshape(1, 896)).astype(BF)
    packed[...] = dot(perm[...], normed).astype(BF).reshape(16, 16, 896)

    def post(k, _):
        o = (m + k) % 16
        rcopy(packed.at[o], inb.at[m], a_send.at[o], a_recv.at[m], (s, o, d)).start()
        return 0

    lax.fori_loop(1, 16, post, 0)
    inb[m] = packed[m]

    def third(t, _):
        for a in range(2):
            i, j = at(a)
            p = pid(a, (i + t) % 4, (j + 2) % 4)
            got_piece(p, a, 0)
            got_piece(p, a, 1)
            share(p, a)
        return 0

    lax.fori_loop(0, 4, third, 0)
    for cp in own_q + own_kv + [own_n]:
        cp.wait()

    def arrive(k, _):
        o = (m + k) % 16
        rcopy(packed.at[o], inb.at[o], a_send.at[o], a_recv.at[o], (s, o, d)).wait()
        return 0

    lax.fori_loop(1, 16, arrive, 0)
    qkv[...] = dot(inb[...].reshape(256, 896), wqkv[...]).astype(BF).reshape(16, 16, 1280)
    kbuf[:, 192:208, :] = qkv[:, :, 768:1024]
    vbuf[:, 192:208, :] = qkv[:, :, 1024:1280]

    factor = 128 ** (-0.5)

    def give(h, g):
        return rcopy(outb.at[h, g], retb.at[h, m], r_send.at[h, g], r_recv.at[h, m], (s, g, d))

    for h in range(2):
        kcols = slice(h * 128, (h + 1) * 128)
        for q4 in range(4):
            group = range(q4 * 4, q4 * 4 + 4)
            sc = []
            for g in group:
                q = [qkv[g, :, (h * 3 + e) * 128 : (h * 3 + e + 1) * 128] for e in range(3)]
                sc.append(dot_t(jnp.concatenate(q, axis=0), kbuf[g, :, kcols]).reshape(3, 16, 208))
            sc = jnp.stack(sc) * factor + bias[q4 * 4 : q4 * 4 + 4][:, None]
            pr = jnp.exp(sc - jnp.max(sc, axis=-1, keepdims=True))
            inv = (1.0 / jnp.sum(pr, axis=-1, keepdims=True)).reshape(4, 48, 1)
            pr = pr.astype(BF).reshape(4, 48, 208)
            for gg, g in enumerate(group):
                o = (dot(pr[gg], vbuf[g, :, kcols]) * inv[gg]).astype(BF)
                for e in range(3):
                    outb[h, g, :, e * 128 : (e + 1) * 128] = o[e * 16 : (e + 1) * 16]

            def give4(g, _):
                @pl.when(g != m)
                def _():
                    give(h, g).start()

                return 0

            lax.fori_loop(q4 * 4, q4 * 4 + 4, give4, 0)
        retb[h, m] = outb[h, m]
    swaps = []
    for h in range(2):

        def back(k, _):
            o = (m + k) % 16
            rcopy(outb.at[h, o], retb.at[h, o], r_send.at[h, o], r_recv.at[h, o], (s, o, d)).wait()
            return 0

        lax.fori_loop(1, 16, back, 0)
        mine[h] = dot(perm_t[...], retb[h].reshape(256, 384)).astype(BF)
        swaps.append(rcopy(mine.at[h], part.at[h], x_send.at[h], x_recv.at[h], zdev(4)))
        swaps[h].start()

    def shared(t, _):
        p = (m + t) % 16
        for a in range(2):
            dst = er.at[p, 1 - c, a]
            rcopy(dst, dst, fs_send.at[p, a], fs_recv.at[p, a], sib).wait_recv()
            full(p, a, fs_send.at[p, a], fs_recv.at[p, a], sib).wait_send()
        return 0

    lax.fori_loop(1, 16, shared, 0)

    def early(t, _):
        e = er[pl.ds(t * 2, 2), :, :, :, 0:1024].reshape(256, 1024)
        hpre[t] = dot_t(noisy[...], e)
        return 0

    lax.fori_loop(0, 8, early, 0)
    swaps[0].wait()

    def late0(t, _):
        e = er[pl.ds(t * 2, 2), :, :, :, 1024:1408].reshape(256, 384)
        hpre[t] += dot_t(part[0], e)
        return 0

    lax.fori_loop(0, 8, late0, 0)
    swaps[1].wait()

    def late1(t, _):
        e = er[pl.ds(t * 2, 2), :, :, :, 1408:EXP].reshape(256, 384)
        hact[t] = jax.nn.gelu(hpre[t] + dot_t(part[1], e)).astype(BF)
        return 0

    lax.fori_loop(0, 8, late1, 0)
    h = jnp.concatenate([hact[t] for t in range(8)], axis=1)
    for n in range(4):
        cols = slice(n * 256, (n + 1) * 256)
        r = er[:, :, :, :, EXP + n * 256 : EXP + (n + 1) * 256].reshape(2048, 256)
        out_ref[:, cols] = (noisy[:, cols].astype(F32) + 0.5 * dot(h, r)).astype(BF)

    for cp in sends:
        cp.wait_send()
    for zi in (zm, zp, z2):
        for hh in range(2):
            dst = wbuf.at[zi, c, hh]
            rcopy(dst, dst, ts_send.at[zi, hh], t_recv.at[zi, c, hh], sib).wait_send()

    def sent(i, _):
        for a in range(2):
            p = pid(a, i, at(a)[1])
            for k in range(2):
                full(p, a, f_send2.at[a, i, k], f_recv.at[p, a, 0], sib).wait_send()
                piece(p, a, k, f_fwd2.at[a, i, k], sib).wait_send()
        return 0

    lax.fori_loop(0, 4, sent, 0)


def shards(hidden, owner, w, gain, wq, wk, wv, cache, fill, noisy, fe, fr):
    any_ = pl.BlockSpec(memory_space=pl.ANY)
    vmem = pl.BlockSpec(memory_space=pltpu.VMEM)
    dma = pltpu.SemaphoreType.DMA
    return pl.pallas_call(
        kernel,
        out_shape=jax.ShapeDtypeStruct((128, 1024), BF),
        in_specs=[any_, any_, any_, vmem, any_, any_, any_, any_, any_, any_, any_, any_],
        out_specs=vmem,
        scratch_shapes=[
            pltpu.SMEM((32,), jnp.int32),
            pltpu.SMEM((64,), jnp.int32),
            pltpu.VMEM((4, 128, 896), BF),
            pltpu.VMEM((4, 2, 2, 224, 896), BF),
            pltpu.VMEM((896, 1280), BF),
            pltpu.VMEM((16, 208, 256), BF),
            pltpu.VMEM((16, 208, 256), BF),
            pltpu.VMEM((128, 1024), BF),
            pltpu.VMEM((16, 2, 2, 32, HID), BF),
            pltpu.VMEM((16, 16, 208), F32),
            pltpu.VMEM((256, 128), BF),
            pltpu.VMEM((128, 256), BF),
            pltpu.VMEM((128, 896), F32),
            pltpu.VMEM((16, 16, 896), BF),
            pltpu.VMEM((16, 16, 896), BF),
            pltpu.VMEM((16, 16, 1280), BF),
            pltpu.VMEM((2, 16, 16, 384), BF),
            pltpu.VMEM((2, 16, 16, 384), BF),
            pltpu.VMEM((2, 128, 384), BF),
            pltpu.VMEM((2, 128, 384), BF),
            pltpu.VMEM((8, 128, 256), F32),
            pltpu.VMEM((8, 128, 256), BF),
            dma((32,)),
            dma((6,)),
            dma((4, 2, 2)),
            dma((4, 2)),
            dma((2, 2)),
            dma((2, 4, 2)),
            dma((2, 2)),
            dma((2, 4, 2)),
            dma((16, 2, 2)),
            dma((16, 2)),
            dma((16, 2)),
            dma((16,)),
            dma((16,)),
            dma((2, 16)),
            dma((2, 16)),
            dma((2,)),
            dma((2,)),
        ],
        compiler_params=pltpu.CompilerParams(
            collective_id=0, has_side_effects=True, vmem_limit_bytes=63 * 2**20
        ),
        name="talker_flow",
    )(
        hidden, owner, w, gain, wq, wk, wv, cache.reshape(16, 4, 2, 48, 256), fill, noisy, fe, fr,
    )


def solution(mesh):
    placed = (
        P(("segment", "mp", "dp"), None),
        P(("segment", "mp", "dp")),
        P("dp", None),
        P(),
        P(),
        P(),
        P(),
        P(("segment", "mp", "dp"), None, None, None),
        P(("segment", "mp", "dp")),
        P(("segment", "mp", "dp"), None),
        P("mp", None),
        P("mp", None),
    )
    return jax.shard_map(
        shards,
        mesh=mesh,
        in_specs=placed,
        out_specs=P(("segment", "mp", "dp"), None),
        check_vma=False,
    )
```

```python
import jax
import jax.numpy as jnp
from jax import lax
from jax.experimental import pallas as pl
from jax.experimental.pallas import tpu as pltpu
from jax.sharding import PartitionSpec as P

MESH = pl.DeviceIdType.MESH
BF = jnp.bfloat16
F32 = jnp.float32
NEG = -1e30
EXP = 1792


def dot(a, b):
    return jnp.dot(a, b, preferred_element_type=F32)


def dot_t(a, b):
    return lax.dot_general(a, b, (((1,), (1,)), ((), ())), preferred_element_type=F32)


def kernel(
    hid_ref, own_hbm, w_ref, gain_ref, wq_ref, wk_ref, wv_ref, kv_ref, len_hbm, noisy_ref, fe_ref, fr_ref,
    out_ref,
    own_ref, len_ref, hid, hin, pout, pin, wown, wqkv, kbuf, vbuf, noisy, eb, rb, bias, perm, perm_t, pacc, packed, inb, qkv, outb, retb, mine, part, hpre, hact,
    lsem, w_send, w_recv, h_send, h_recv, p_send, p_recv, f_send1, f_send2, f_fwd1, f_fwd2, f_recv, fs_send, fs_recv,
    a_send, a_recv, r_send, r_recv, x_send, x_recv,
):
    s = lax.axis_index("segment")
    m = lax.axis_index("mp")
    d = lax.axis_index("dp")
    zl, c = d // 2, d % 2
    z = s * 4 + zl
    y, x = m // 4, m % 4
    sib = (s, m, zl * 2 + (1 - c))

    def zdev(dz):
        zz = (z + dz + 8) % 8
        return (zz // 4, m, (zz % 4) * 2 + c)

    def xydev(dx, dy):
        return (s, ((y + dy + 4) % 4) * 4 + (x + dx + 4) % 4, d)

    def rcopy(src, dst, ss, rs, dev):
        return pltpu.make_async_remote_copy(
            src_ref=src, dst_ref=dst, send_sem=ss, recv_sem=rs, device_id=dev, device_id_type=MESH
        )

    barrier = pltpu.get_barrier_semaphore()

    def greet(k, _):
        pl.semaphore_signal(barrier, inc=1, device_id=(s, (m + k) % 16, d), device_id_type=MESH)
        return 0

    for dev in (zdev(1), zdev(-1), zdev(2), zdev(-2), zdev(4), sib):
        pl.semaphore_signal(barrier, inc=1, device_id=dev, device_id_type=MESH)
    lax.fori_loop(1, 16, greet, 0)

    local = []

    def load(src, dst):
        cp = pltpu.make_async_copy(src, dst, lsem.at[len(local)])
        cp.start()
        local.append(cp)
        return cp

    own_s = [load(own_hbm, own_ref), load(len_hbm, len_ref)]
    own_e = []
    for cc in range(2):
        for a in range(2):
            rows = pl.ds(cc * 64 + a * 32, 32)
            own_e.append(load(fe_ref.at[rows], eb.at[m, cc, a]))
            own_e.append(load(fr_ref.at[rows], rb.at[m, cc, a]))
    own_w = load(w_ref, wown.at[c])
    own_h = load(hid_ref.at[:, pl.ds(pl.multiple_of(zl * 896, 128), 896)], hid)
    own_q = [
        load(wq_ref, wqkv.at[:, pl.ds(0, 768)]),
        load(wk_ref, wqkv.at[:, pl.ds(768, 256)]),
        load(wv_ref, wqkv.at[:, pl.ds(1024, 256)]),
    ]
    own_n = load(noisy_ref, noisy)
    own_kv = []
    for i in range(4):
        own_kv.append(load(kv_ref.at[:, i, 0], kbuf.at[:, pl.ds(i * 48, 48)]))
        own_kv.append(load(kv_ref.at[:, i, 1], vbuf.at[:, pl.ds(i * 48, 48)]))

    pl.semaphore_wait(barrier, 21)

    sends = []

    def go(cp):
        cp.start()
        sends.append(cp)

    two = 2 - 4 * c
    steps = (two, 1, -1)

    def hcopy(k, dz):
        cols = pl.ds(pl.multiple_of((zl + dz + 4) % 4 * 896, 128), 896)
        return rcopy(hid_ref.at[:, cols], hin.at[k], h_send.at[k], h_recv.at[k], zdev(dz))

    def pcopy(k, dz):
        return rcopy(pout.at[k], pin.at[k], p_send.at[k], p_recv.at[k], zdev(-dz))

    def own_weight(cc):
        return rcopy(w_ref, wown.at[cc], w_send.at[0], w_recv.at[0], sib)

    for k, dz in enumerate(steps):
        go(hcopy(k, dz))
    go(own_weight(c))

    def pid(a, i, j):
        return j * 4 + i if a == 0 else i * 4 + j

    def nb1(a, k):
        return xydev(k, 0) if a == 0 else xydev(0, k)

    def nb2(a, k):
        return xydev(0, k) if a == 0 else xydev(k, 0)

    def at(a):
        return (x, y) if a == 0 else (y, x)

    class Gather:
        def __init__(self, n, buf):
            self.n, self.buf = n, buf

        def full(self, p, a, ss, rs, dev):
            return rcopy(self.buf.at[p, c, a], self.buf.at[p, c, a], ss, rs, dev)

        def piece(self, p, a, k, ss, dev):
            ref = self.buf.at[p, c, a, pl.ds(k * 16, 16)]
            return rcopy(ref, ref, ss, f_recv.at[self.n, p, a, k], dev)

        def got(self, p, a):
            self.full(p, a, f_send1.at[self.n, 0, 0], f_recv.at[self.n, p, a, 0], sib).wait_recv()

        def got_pieces(self, p, a):
            for k in range(2):
                self.piece(p, a, k, f_send1.at[self.n, 0, 0], sib).wait_recv()

        def share(self, p, a):
            self.full(p, a, fs_send.at[self.n, p, a], fs_recv.at[self.n, p, a], sib).start()

        def spread(self, a, i, j):
            p = pid(a, i, j)
            for k in range(2):
                sems = f_send2.at[self.n, a, i, k], f_recv.at[self.n, p, a, 0]
                self.full(p, a, *sems, nb2(a, 1 - 2 * k)).start()

        def begin(self):
            for a in range(2):
                p = pid(a, *at(a))
                for k in range(2):
                    sems = f_send1.at[self.n, a, k], f_recv.at[self.n, p, a, 0]
                    go(self.full(p, a, *sems, nb1(a, 1 - 2 * k)))

        def begin2(self):
            for a in range(2):
                self.spread(a, *at(a))

        def first(self):
            for a in range(2):
                i, j = at(a)
                for k in range(2):
                    p = pid(a, (i + (3 if k == 0 else 1)) % 4, j)
                    self.got(p, a)
                    go(self.piece(p, a, k, f_fwd1.at[self.n, a, k], nb1(a, 1 - 2 * k)))

        def first_spread(self):
            for a in range(2):
                i, j = at(a)
                for k in (1, 3):
                    self.spread(a, (i + k) % 4, j)
                    self.share(pid(a, (i + k) % 4, j), a)

        def first_far(self):
            for a in range(2):
                i, j = at(a)
                i2 = (i + 2) % 4
                self.got_pieces(pid(a, i2, j), a)
                self.spread(a, i2, j)
                self.share(pid(a, i2, j), a)

        def second(self, lo, hi):
            def step(t, _):
                for a in range(2):
                    i, j = at(a)
                    it = (i + t) % 4
                    for k in range(2):
                        p = pid(a, it, (j + (3 if k == 0 else 1)) % 4)
                        self.got(p, a)
                        self.piece(p, a, k, f_fwd2.at[self.n, a, it, k], nb2(a, 1 - 2 * k)).start()
                        self.share(p, a)
                return 0

            lax.fori_loop(lo, hi, step, 0)

        def second_far(self):
            def step(t, _):
                for a in range(2):
                    i, j = at(a)
                    p = pid(a, (i + t) % 4, (j + 2) % 4)
                    self.got_pieces(p, a)
                    self.share(p, a)
                return 0

            lax.fori_loop(0, 4, step, 0)

        def shared(self):
            def step(t, _):
                p = (m + t) % 16
                for a in range(2):
                    dst = self.buf.at[p, 1 - c, a]
                    rcopy(dst, dst, fs_send.at[self.n, p, a], fs_recv.at[self.n, p, a], sib).wait_recv()
                return 0

            lax.fori_loop(1, 16, step, 0)

        def sent(self):
            def step(i, _):
                for a in range(2):
                    p = pid(a, i, at(a)[1])
                    for k in range(2):
                        self.full(p, a, f_send2.at[self.n, a, i, k], f_recv.at[self.n, p, a, 0], sib).wait_send()
                        self.piece(p, a, k, f_fwd2.at[self.n, a, i, k], sib).wait_send()
                return 0

            lax.fori_loop(0, 4, step, 0)

            def step2(t, _):
                p = (m + t) % 16
                for a in range(2):
                    self.full(p, a, fs_send.at[self.n, p, a], fs_recv.at[self.n, p, a], sib).wait_send()
                return 0

            lax.fori_loop(1, 16, step2, 0)

    expand, reduce = Gather(0, eb), Gather(1, rb)
    for cp in own_e:
        cp.wait()
    expand.begin()
    expand.begin2()
    expand.first()
    expand.first_spread()
    expand.first_far()
    reduce.begin()
    reduce.begin2()
    for cp in own_s:
        cp.wait()
    r0 = lax.broadcasted_iota(jnp.int32, (16, 208), 0)
    j0 = lax.broadcasted_iota(jnp.int32, (16, 208), 1)
    u0 = j0 - 192
    fresh_ok = (j0 >= 192) & (u0 // 4 == r0 // 4) & (u0 % 4 <= r0 % 4)
    slot0 = j0 // 48
    pos0 = j0 % 48
    same = (j0 < 192) & (slot0 == r0 // 4)

    def make_bias(g, _):
        ln = jnp.zeros((16, 208), jnp.int32)
        for i in range(4):
            ln = jnp.where(slot0 == i, len_ref[g * 4 + i], ln)
        ok = fresh_ok | (same & (pos0 < ln))
        bias[g] = jnp.where(ok, 0.0, NEG)
        return 0

    lax.fori_loop(0, 16, make_bias, 0)

    ri = lax.broadcasted_iota(jnp.int32, (128, 128), 0)
    ci = lax.broadcasted_iota(jnp.int32, (128, 128), 1)

    def owners(k, carry):
        a, b = carry
        o = own_ref[k]
        return jnp.where(ri // 4 == k, o, a), jnp.where(ci // 4 == k, o, b)

    zero = jnp.zeros((128, 128), jnp.int32)
    own_rows, own_cols = lax.fori_loop(0, 32, owners, (zero, zero))
    eq = own_rows == own_cols
    rank_row = jnp.sum(jnp.where(eq & (ri // 4 < ci // 4) & (ri % 4 == 0), 1.0, 0.0), axis=0, keepdims=True)
    rank_col = jnp.sum(jnp.where(eq & (ci // 4 < ri // 4) & (ci % 4 == 0), 1.0, 0.0), axis=1, keepdims=True)
    tgt_row = own_cols[0:1, :] * 16 + rank_row.astype(jnp.int32) * 4 + ci[0:1, :] % 4
    tgt_col = own_rows[:, 0:1] * 16 + rank_col.astype(jnp.int32) * 4 + ri[:, 0:1] % 4
    perm[...] = jnp.where(lax.broadcasted_iota(jnp.int32, (256, 128), 0) == tgt_row, 1.0, 0.0).astype(BF)
    perm_t[...] = jnp.where(lax.broadcasted_iota(jnp.int32, (128, 256), 1) == tgt_col, 1.0, 0.0).astype(BF)

    own_w.wait()
    own_weight(1 - c).wait_recv()
    wt = wown[...].reshape(896, 896)
    for k in (1, 2, 0):
        hcopy(k, steps[k]).wait_recv()
        pout[k] = dot(hin[k], wt).astype(BF)
        go(pcopy(k, steps[k]))
    own_h.wait()
    pacc[...] = dot(hid[...], wt)
    expand.second(0, 4)
    reduce.first()
    for k in range(3):
        pcopy(k, steps[k]).wait_recv()
    projected = pacc[...] + pin[0].astype(F32) + pin[1].astype(F32) + pin[2].astype(F32)
    projected = projected.astype(BF).astype(F32)
    scale = lax.rsqrt(jnp.mean(projected * projected, axis=-1, keepdims=True) + 1e-06)
    normed = (projected * scale * gain_ref[...].astype(F32).reshape(1, 896)).astype(BF)
    packed[...] = dot(perm[...], normed).astype(BF).reshape(16, 16, 896)

    def post(k, _):
        o = (m + k) % 16
        rcopy(packed.at[o], inb.at[m], a_send.at[o], a_recv.at[m], (s, o, d)).start()
        return 0

    lax.fori_loop(1, 16, post, 0)
    inb[m] = packed[m]

    expand.second_far()
    for cp in own_q + own_kv + [own_n]:
        cp.wait()

    def arrive(k, _):
        o = (m + k) % 16
        rcopy(packed.at[o], inb.at[o], a_send.at[o], a_recv.at[o], (s, o, d)).wait()
        return 0

    lax.fori_loop(1, 16, arrive, 0)
    reduce.first_spread()
    reduce.first_far()
    qkv[...] = dot(inb[...].reshape(256, 896), wqkv[...]).astype(BF).reshape(16, 16, 1280)
    kbuf[:, 192:208, :] = qkv[:, :, 768:1024]
    vbuf[:, 192:208, :] = qkv[:, :, 1024:1280]

    factor = 128 ** (-0.5)

    def give(h, g):
        return rcopy(outb.at[h, g], retb.at[h, m], r_send.at[h, g], r_recv.at[h, m], (s, g, d))

    for h in range(2):
        kcols = slice(h * 128, (h + 1) * 128)
        for q4 in range(4):
            group = range(q4 * 4, q4 * 4 + 4)
            sc = []
            for g in group:
                q = [qkv[g, :, (h * 3 + e) * 128 : (h * 3 + e + 1) * 128] for e in range(3)]
                sc.append(dot_t(jnp.concatenate(q, axis=0), kbuf[g, :, kcols]).reshape(3, 16, 208))
            sc = jnp.stack(sc) * factor + bias[q4 * 4 : q4 * 4 + 4][:, None]
            pr = jnp.exp(sc - jnp.max(sc, axis=-1, keepdims=True))
            inv = (1.0 / jnp.sum(pr, axis=-1, keepdims=True)).reshape(4, 48, 1)
            pr = pr.astype(BF).reshape(4, 48, 208)
            for gg, g in enumerate(group):
                o = (dot(pr[gg], vbuf[g, :, kcols]) * inv[gg]).astype(BF)
                for e in range(3):
                    outb[h, g, :, e * 128 : (e + 1) * 128] = o[e * 16 : (e + 1) * 16]

            def give4(g, _):
                @pl.when(g != m)
                def _():
                    give(h, g).start()

                return 0

            lax.fori_loop(q4 * 4, q4 * 4 + 4, give4, 0)
        retb[h, m] = outb[h, m]
    reduce.second(0, 1)
    swaps = []
    for h in range(2):

        def back(k, _):
            o = (m + k) % 16
            rcopy(outb.at[h, o], retb.at[h, o], r_send.at[h, o], r_recv.at[h, o], (s, o, d)).wait()
            return 0

        lax.fori_loop(1, 16, back, 0)
        mine[h] = dot(perm_t[...], retb[h].reshape(256, 384)).astype(BF)
        swaps.append(rcopy(mine.at[h], part.at[h], x_send.at[h], x_recv.at[h], zdev(4)))
        swaps[h].start()
        if h == 0:
            reduce.second(1, 4)

    expand.shared()

    for t in range(8):
        e = eb[2 * t : 2 * t + 2, :, :, :, 0:1024].reshape(256, 1024)
        hpre[t] = dot_t(noisy[...], e)

    reduce.second_far()
    swaps[0].wait()

    for t in range(8):
        e = eb[2 * t : 2 * t + 2, :, :, :, 1024:1408].reshape(256, 384)
        hpre[t] += dot_t(part[0], e)

    swaps[1].wait()

    for t in range(8):
        e = eb[2 * t : 2 * t + 2, :, :, :, 1408:EXP].reshape(256, 384)
        hact[t] = jax.nn.gelu(hpre[t] + dot_t(part[1], e)).astype(BF)

    reduce.shared()
    h = jnp.concatenate([hact[t] for t in range(8)], axis=1)
    for n in range(4):
        cols = slice(n * 256, (n + 1) * 256)
        r = rb[:, :, :, :, cols].reshape(2048, 256)
        out_ref[:, cols] = (noisy[:, cols].astype(F32) + 0.5 * dot(h, r)).astype(BF)

    for cp in sends:
        cp.wait_send()
    expand.sent()
    reduce.sent()


def shards(hidden, owner, w, gain, wq, wk, wv, cache, fill, noisy, fe, fr):
    any_ = pl.BlockSpec(memory_space=pl.ANY)
    vmem = pl.BlockSpec(memory_space=pltpu.VMEM)
    dma = pltpu.SemaphoreType.DMA
    return pl.pallas_call(
        kernel,
        out_shape=jax.ShapeDtypeStruct((128, 1024), BF),
        in_specs=[any_, any_, any_, vmem, any_, any_, any_, any_, any_, any_, any_, any_],
        out_specs=vmem,
        scratch_shapes=[
            pltpu.SMEM((32,), jnp.int32),
            pltpu.SMEM((64,), jnp.int32),
            pltpu.VMEM((128, 896), BF),
            pltpu.VMEM((3, 128, 896), BF),
            pltpu.VMEM((3, 128, 896), BF),
            pltpu.VMEM((3, 128, 896), BF),
            pltpu.VMEM((2, 448, 896), BF),
            pltpu.VMEM((896, 1280), BF),
            pltpu.VMEM((16, 208, 256), BF),
            pltpu.VMEM((16, 208, 256), BF),
            pltpu.VMEM((128, 1024), BF),
            pltpu.VMEM((16, 2, 2, 32, EXP), BF),
            pltpu.VMEM((16, 2, 2, 32, 1024), BF),
            pltpu.VMEM((16, 16, 208), F32),
            pltpu.VMEM((256, 128), BF),
            pltpu.VMEM((128, 256), BF),
            pltpu.VMEM((128, 896), F32),
            pltpu.VMEM((16, 16, 896), BF),
            pltpu.VMEM((16, 16, 896), BF),
            pltpu.VMEM((16, 16, 1280), BF),
            pltpu.VMEM((2, 16, 16, 384), BF),
            pltpu.VMEM((2, 16, 16, 384), BF),
            pltpu.VMEM((2, 128, 384), BF),
            pltpu.VMEM((2, 128, 384), BF),
            pltpu.VMEM((8, 128, 256), F32),
            pltpu.VMEM((8, 128, 256), BF),
            dma((32,)),
            dma((1,)),
            dma((1,)),
            dma((3,)),
            dma((3,)),
            dma((3,)),
            dma((3,)),
            dma((2, 2, 2)),
            dma((2, 2, 4, 2)),
            dma((2, 2, 2)),
            dma((2, 2, 4, 2)),
            dma((2, 16, 2, 2)),
            dma((2, 16, 2)),
            dma((2, 16, 2)),
            dma((16,)),
            dma((16,)),
            dma((2, 16)),
            dma((2, 16)),
            dma((2,)),
            dma((2,)),
        ],
        compiler_params=pltpu.CompilerParams(
            collective_id=0, has_side_effects=True, vmem_limit_bytes=63 * 2**20
        ),
        name="talker_flow",
    )(
        hidden, owner, w, gain, wq, wk, wv, cache.reshape(16, 4, 2, 48, 256), fill, noisy, fe, fr,
    )


def solution(mesh):
    placed = (
        P(("segment", "mp", "dp"), None),
        P(("segment", "mp", "dp")),
        P("dp", None),
        P(),
        P(),
        P(),
        P(),
        P(("segment", "mp", "dp"), None, None, None),
        P(("segment", "mp", "dp")),
        P(("segment", "mp", "dp"), None),
        P("mp", None),
        P("mp", None),
    )
    return jax.shard_map(
        shards,
        mesh=mesh,
        in_specs=placed,
        out_specs=P(("segment", "mp", "dp"), None),
        check_vma=False,
    )
```

```python
import jax
import jax.numpy as jnp
from jax import lax
from jax.experimental import pallas as pl
from jax.experimental.pallas import tpu as pltpu
from jax.sharding import PartitionSpec as P

MESH = pl.DeviceIdType.MESH
BF = jnp.bfloat16
F32 = jnp.float32
NEG = -1e30
EXP = 1792


def dot(a, b):
    return jnp.dot(a, b, preferred_element_type=F32)


def dot_t(a, b):
    return lax.dot_general(a, b, (((1,), (1,)), ((), ())), preferred_element_type=F32)


def kernel(
    hid_ref, own_hbm, w_ref, gain_ref, wq_ref, wk_ref, wv_ref, kv_ref, len_hbm, noisy_ref, fe_ref, fr_ref,
    out_ref,
    own_ref, len_ref, hid, hin, pout0, pout1, pin0, pin1, wown, wqkv, kbuf, vbuf, noisy, eb, rb, bias, perm, perm_t, pacc, packed0, packed1, inb0, inb1, qkv, outb, retb, mine, part, hpre, hact,
    lsem, w_send, w_recv, h_send, h_recv, p_send, p_recv, f_send1, f_send2, f_fwd1, f_fwd2, f_recv, fs_send, fs_recv,
    a_send, a_recv, r_send, r_recv, x_send, x_recv,
):
    s = lax.axis_index("segment")
    m = lax.axis_index("mp")
    d = lax.axis_index("dp")
    zl, c = d // 2, d % 2
    z = s * 4 + zl
    y, x = m // 4, m % 4
    sib = (s, m, zl * 2 + (1 - c))

    def zdev(dz):
        zz = (z + dz + 8) % 8
        return (zz // 4, m, (zz % 4) * 2 + c)

    def xydev(dx, dy):
        return (s, ((y + dy + 4) % 4) * 4 + (x + dx + 4) % 4, d)

    def rcopy(src, dst, ss, rs, dev):
        return pltpu.make_async_remote_copy(
            src_ref=src, dst_ref=dst, send_sem=ss, recv_sem=rs, device_id=dev, device_id_type=MESH
        )

    barrier = pltpu.get_barrier_semaphore()

    def greet(k, _):
        pl.semaphore_signal(barrier, inc=1, device_id=(s, (m + k) % 16, d), device_id_type=MESH)
        return 0

    for dev in (zdev(1), zdev(-1), zdev(2), zdev(-2), zdev(4), sib):
        pl.semaphore_signal(barrier, inc=1, device_id=dev, device_id_type=MESH)
    lax.fori_loop(1, 16, greet, 0)

    local = []

    def load(src, dst):
        cp = pltpu.make_async_copy(src, dst, lsem.at[len(local)])
        cp.start()
        local.append(cp)
        return cp

    own_s = [load(own_hbm, own_ref), load(len_hbm, len_ref)]
    own_e = []
    for cc in range(2):
        for a in range(2):
            rows = pl.ds(cc * 64 + a * 32, 32)
            own_e.append(load(fe_ref.at[rows], eb.at[m, cc, a]))
            own_e.append(load(fr_ref.at[rows], rb.at[m, cc, a]))
    own_w = load(w_ref, wown.at[c])
    own_h = load(hid_ref.at[:, pl.ds(pl.multiple_of(zl * 896, 128), 896)], hid)
    own_q = [
        load(wq_ref, wqkv.at[:, pl.ds(0, 768)]),
        load(wk_ref, wqkv.at[:, pl.ds(768, 256)]),
        load(wv_ref, wqkv.at[:, pl.ds(1024, 256)]),
    ]
    own_n = load(noisy_ref, noisy)
    own_kv = []
    for i in range(4):
        own_kv.append(load(kv_ref.at[:, i, 0], kbuf.at[:, pl.ds(i * 48, 48)]))
        own_kv.append(load(kv_ref.at[:, i, 1], vbuf.at[:, pl.ds(i * 48, 48)]))

    pl.semaphore_wait(barrier, 21)

    sends = []

    def go(cp):
        cp.start()
        sends.append(cp)

    two = 2 - 4 * c
    steps = (1, -1, two)

    def hcopy(k, dz):
        cols = pl.ds(pl.multiple_of((zl + dz + 4) % 4 * 896, 128), 896)
        return rcopy(hid_ref.at[:, cols], hin.at[k], h_send.at[k], h_recv.at[k], zdev(dz))

    halves = ((pout0, pin0, packed0, inb0, slice(0, 512)), (pout1, pin1, packed1, inb1, slice(512, 896)))

    def pcopy(n, k, dz):
        return rcopy(halves[n][0].at[k], halves[n][1].at[k], p_send.at[n, k], p_recv.at[n, k], zdev(-dz))

    def own_weight(cc):
        return rcopy(w_ref, wown.at[cc], w_send.at[0], w_recv.at[0], sib)

    for k, dz in enumerate(steps):
        go(hcopy(k, dz))
    go(own_weight(c))

    def pid(a, i, j):
        return j * 4 + i if a == 0 else i * 4 + j

    def nb1(a, k):
        return xydev(k, 0) if a == 0 else xydev(0, k)

    def nb2(a, k):
        return xydev(0, k) if a == 0 else xydev(k, 0)

    def at(a):
        return (x, y) if a == 0 else (y, x)

    class Gather:
        def __init__(self, n, buf):
            self.n, self.buf = n, buf

        def full(self, p, a, ss, rs, dev):
            return rcopy(self.buf.at[p, c, a], self.buf.at[p, c, a], ss, rs, dev)

        def piece(self, p, a, k, ss, dev):
            ref = self.buf.at[p, c, a, pl.ds(k * 16, 16)]
            return rcopy(ref, ref, ss, f_recv.at[self.n, p, a, k], dev)

        def got(self, p, a):
            self.full(p, a, f_send1.at[self.n, 0, 0], f_recv.at[self.n, p, a, 0], sib).wait_recv()

        def got_pieces(self, p, a):
            for k in range(2):
                self.piece(p, a, k, f_send1.at[self.n, 0, 0], sib).wait_recv()

        def share(self, p, a):
            self.full(p, a, fs_send.at[self.n, p, a], fs_recv.at[self.n, p, a], sib).start()

        def spread(self, a, i, j):
            p = pid(a, i, j)
            for k in range(2):
                sems = f_send2.at[self.n, a, i, k], f_recv.at[self.n, p, a, 0]
                self.full(p, a, *sems, nb2(a, 1 - 2 * k)).start()

        def begin(self):
            for a in range(2):
                p = pid(a, *at(a))
                for k in range(2):
                    sems = f_send1.at[self.n, a, k], f_recv.at[self.n, p, a, 0]
                    go(self.full(p, a, *sems, nb1(a, 1 - 2 * k)))

        def begin2(self):
            for a in range(2):
                self.spread(a, *at(a))

        def first(self):
            for a in range(2):
                i, j = at(a)
                for k in range(2):
                    p = pid(a, (i + (3 if k == 0 else 1)) % 4, j)
                    self.got(p, a)
                    go(self.piece(p, a, k, f_fwd1.at[self.n, a, k], nb1(a, 1 - 2 * k)))

        def first_spread(self):
            for a in range(2):
                i, j = at(a)
                for k in (1, 3):
                    self.spread(a, (i + k) % 4, j)
                    self.share(pid(a, (i + k) % 4, j), a)

        def first_far(self):
            for a in range(2):
                i, j = at(a)
                i2 = (i + 2) % 4
                self.got_pieces(pid(a, i2, j), a)
                self.spread(a, i2, j)
                self.share(pid(a, i2, j), a)

        def second(self, lo, hi):
            def step(t, _):
                for a in range(2):
                    i, j = at(a)
                    it = (i + t) % 4
                    for k in range(2):
                        p = pid(a, it, (j + (3 if k == 0 else 1)) % 4)
                        self.got(p, a)
                        self.piece(p, a, k, f_fwd2.at[self.n, a, it, k], nb2(a, 1 - 2 * k)).start()
                        self.share(p, a)
                return 0

            lax.fori_loop(lo, hi, step, 0)

        def second_far(self):
            def step(t, _):
                for a in range(2):
                    i, j = at(a)
                    p = pid(a, (i + t) % 4, (j + 2) % 4)
                    self.got_pieces(p, a)
                    self.share(p, a)
                return 0

            lax.fori_loop(0, 4, step, 0)

        def shared(self):
            def step(t, _):
                p = (m + t) % 16
                for a in range(2):
                    dst = self.buf.at[p, 1 - c, a]
                    rcopy(dst, dst, fs_send.at[self.n, p, a], fs_recv.at[self.n, p, a], sib).wait_recv()
                return 0

            lax.fori_loop(1, 16, step, 0)

        def sent(self):
            def step(i, _):
                for a in range(2):
                    p = pid(a, i, at(a)[1])
                    for k in range(2):
                        self.full(p, a, f_send2.at[self.n, a, i, k], f_recv.at[self.n, p, a, 0], sib).wait_send()
                        self.piece(p, a, k, f_fwd2.at[self.n, a, i, k], sib).wait_send()
                return 0

            lax.fori_loop(0, 4, step, 0)

            def step2(t, _):
                p = (m + t) % 16
                for a in range(2):
                    self.full(p, a, fs_send.at[self.n, p, a], fs_recv.at[self.n, p, a], sib).wait_send()
                return 0

            lax.fori_loop(1, 16, step2, 0)

    expand, reduce = Gather(0, eb), Gather(1, rb)
    for cp in own_e:
        cp.wait()
    expand.begin()
    expand.begin2()
    expand.first()
    expand.first_spread()
    reduce.begin()
    reduce.begin2()
    own_w.wait()
    own_weight(1 - c).wait_recv()
    wt = wown[...].reshape(896, 896)

    def partial(n, k):
        pout, cols = halves[n][0], halves[n][4]
        pout[k] = dot(hin[k], wt[:, cols]).astype(BF)
        go(pcopy(n, k, steps[k]))

    for k in range(2):
        hcopy(k, steps[k]).wait_recv()
        partial(0, k)
    expand.first_far()
    hcopy(2, steps[2]).wait_recv()
    partial(0, 2)
    for k in range(3):
        partial(1, k)
    own_h.wait()
    pacc[...] = dot(hid[...], wt)

    for cp in own_s:
        cp.wait()
    r0 = lax.broadcasted_iota(jnp.int32, (16, 208), 0)
    j0 = lax.broadcasted_iota(jnp.int32, (16, 208), 1)
    u0 = j0 - 192
    fresh_ok = (j0 >= 192) & (u0 // 4 == r0 // 4) & (u0 % 4 <= r0 % 4)
    slot0 = j0 // 48
    pos0 = j0 % 48
    same = (j0 < 192) & (slot0 == r0 // 4)

    def make_bias(g, _):
        ln = jnp.zeros((16, 208), jnp.int32)
        for i in range(4):
            ln = jnp.where(slot0 == i, len_ref[g * 4 + i], ln)
        ok = fresh_ok | (same & (pos0 < ln))
        bias[g] = jnp.where(ok, 0.0, NEG)
        return 0

    lax.fori_loop(0, 16, make_bias, 0)

    ri = lax.broadcasted_iota(jnp.int32, (128, 128), 0)
    ci = lax.broadcasted_iota(jnp.int32, (128, 128), 1)

    def owners(k, carry):
        a, b = carry
        o = own_ref[k]
        return jnp.where(ri // 4 == k, o, a), jnp.where(ci // 4 == k, o, b)

    zero = jnp.zeros((128, 128), jnp.int32)
    own_rows, own_cols = lax.fori_loop(0, 32, owners, (zero, zero))
    eq = own_rows == own_cols
    rank_row = jnp.sum(jnp.where(eq & (ri // 4 < ci // 4) & (ri % 4 == 0), 1.0, 0.0), axis=0, keepdims=True)
    rank_col = jnp.sum(jnp.where(eq & (ci // 4 < ri // 4) & (ci % 4 == 0), 1.0, 0.0), axis=1, keepdims=True)
    tgt_row = own_cols[0:1, :] * 16 + rank_row.astype(jnp.int32) * 4 + ci[0:1, :] % 4
    tgt_col = own_rows[:, 0:1] * 16 + rank_col.astype(jnp.int32) * 4 + ri[:, 0:1] % 4
    perm[...] = jnp.where(lax.broadcasted_iota(jnp.int32, (256, 128), 0) == tgt_row, 1.0, 0.0).astype(BF)
    perm_t[...] = jnp.where(lax.broadcasted_iota(jnp.int32, (128, 256), 1) == tgt_col, 1.0, 0.0).astype(BF)

    expand.second(0, 4)
    reduce.first()

    for n in range(2):
        _, pin, packed, inb, cols = halves[n]
        for k in range(3):
            pcopy(n, k, steps[k]).wait_recv()
        projected = pacc[:, cols] + pin[0].astype(F32) + pin[1].astype(F32) + pin[2].astype(F32)
        packed[...] = dot(perm[...], projected.astype(BF)).astype(BF).reshape(16, 16, -1)

        def post(k, _):
            o = (m + k) % 16
            rcopy(packed.at[o], inb.at[m], a_send.at[n, o], a_recv.at[n, m], (s, o, d)).start()
            return 0

        lax.fori_loop(1, 16, post, 0)
        inb[m] = packed[m]

    for cp in own_q + own_kv + [own_n]:
        cp.wait()

    for n in range(2):
        _, _, packed, inb, _ = halves[n]

        def arrive(k, _):
            o = (m + k) % 16
            rcopy(packed.at[o], inb.at[o], a_send.at[n, o], a_recv.at[n, o], (s, o, d)).wait()
            return 0

        lax.fori_loop(1, 16, arrive, 0)
    expand.second_far()
    reduce.first_spread()
    reduce.first_far()
    rows = jnp.concatenate([inb0[...].reshape(256, 512), inb1[...].reshape(256, 384)], axis=1).astype(F32)
    scale = lax.rsqrt(jnp.mean(rows * rows, axis=-1, keepdims=True) + 1e-06)
    normed = (rows * scale * gain_ref[...].astype(F32).reshape(1, 896)).astype(BF)
    qkv[...] = dot(normed, wqkv[...]).astype(BF).reshape(16, 16, 1280)
    kbuf[:, 192:208, :] = qkv[:, :, 768:1024]
    vbuf[:, 192:208, :] = qkv[:, :, 1024:1280]

    factor = 128 ** (-0.5)

    def give(h, g):
        return rcopy(outb.at[h, g], retb.at[h, m], r_send.at[h, g], r_recv.at[h, m], (s, g, d))

    for h in range(2):
        kcols = slice(h * 128, (h + 1) * 128)
        for q4 in range(4):
            group = range(q4 * 4, q4 * 4 + 4)
            sc = []
            for g in group:
                q = [qkv[g, :, (h * 3 + e) * 128 : (h * 3 + e + 1) * 128] for e in range(3)]
                sc.append(dot_t(jnp.concatenate(q, axis=0), kbuf[g, :, kcols]).reshape(3, 16, 208))
            sc = jnp.stack(sc) * factor + bias[q4 * 4 : q4 * 4 + 4][:, None]
            pr = jnp.exp(sc - jnp.max(sc, axis=-1, keepdims=True))
            inv = (1.0 / jnp.sum(pr, axis=-1, keepdims=True)).reshape(4, 48, 1)
            pr = pr.astype(BF).reshape(4, 48, 208)
            for gg, g in enumerate(group):
                o = (dot(pr[gg], vbuf[g, :, kcols]) * inv[gg]).astype(BF)
                for e in range(3):
                    outb[h, g, :, e * 128 : (e + 1) * 128] = o[e * 16 : (e + 1) * 16]

            def give4(g, _):
                @pl.when(g != m)
                def _():
                    give(h, g).start()

                return 0

            lax.fori_loop(q4 * 4, q4 * 4 + 4, give4, 0)
        retb[h, m] = outb[h, m]
    reduce.second(0, 1)
    swaps = []
    for h in range(2):

        def back(k, _):
            o = (m + k) % 16
            rcopy(outb.at[h, o], retb.at[h, o], r_send.at[h, o], r_recv.at[h, o], (s, o, d)).wait()
            return 0

        lax.fori_loop(1, 16, back, 0)
        mine[h] = dot(perm_t[...], retb[h].reshape(256, 384)).astype(BF)
        swaps.append(rcopy(mine.at[h], part.at[h], x_send.at[h], x_recv.at[h], zdev(4)))
        swaps[h].start()
        if h == 0:
            reduce.second(1, 4)

    expand.shared()

    for t in range(8):
        e = eb[2 * t : 2 * t + 2, :, :, :, 0:1024].reshape(256, 1024)
        hpre[t] = dot_t(noisy[...], e)

    reduce.second_far()
    swaps[0].wait()

    for t in range(8):
        e = eb[2 * t : 2 * t + 2, :, :, :, 1024:1408].reshape(256, 384)
        hpre[t] += dot_t(part[0], e)

    swaps[1].wait()

    for t in range(8):
        e = eb[2 * t : 2 * t + 2, :, :, :, 1408:EXP].reshape(256, 384)
        hact[t] = jax.nn.gelu(hpre[t] + dot_t(part[1], e)).astype(BF)

    reduce.shared()
    h = jnp.concatenate([hact[t] for t in range(8)], axis=1)
    for n in range(4):
        cols = slice(n * 256, (n + 1) * 256)
        r = rb[:, :, :, :, cols].reshape(2048, 256)
        out_ref[:, cols] = (noisy[:, cols].astype(F32) + 0.5 * dot(h, r)).astype(BF)

    for cp in sends:
        cp.wait_send()
    expand.sent()
    reduce.sent()


def shards(hidden, owner, w, gain, wq, wk, wv, cache, fill, noisy, fe, fr):
    any_ = pl.BlockSpec(memory_space=pl.ANY)
    vmem = pl.BlockSpec(memory_space=pltpu.VMEM)
    dma = pltpu.SemaphoreType.DMA
    return pl.pallas_call(
        kernel,
        out_shape=jax.ShapeDtypeStruct((128, 1024), BF),
        in_specs=[any_, any_, any_, vmem, any_, any_, any_, any_, any_, any_, any_, any_],
        out_specs=vmem,
        scratch_shapes=[
            pltpu.SMEM((32,), jnp.int32),
            pltpu.SMEM((64,), jnp.int32),
            pltpu.VMEM((128, 896), BF),
            pltpu.VMEM((3, 128, 896), BF),
            pltpu.VMEM((3, 128, 512), BF),
            pltpu.VMEM((3, 128, 384), BF),
            pltpu.VMEM((3, 128, 512), BF),
            pltpu.VMEM((3, 128, 384), BF),
            pltpu.VMEM((2, 448, 896), BF),
            pltpu.VMEM((896, 1280), BF),
            pltpu.VMEM((16, 208, 256), BF),
            pltpu.VMEM((16, 208, 256), BF),
            pltpu.VMEM((128, 1024), BF),
            pltpu.VMEM((16, 2, 2, 32, EXP), BF),
            pltpu.VMEM((16, 2, 2, 32, 1024), BF),
            pltpu.VMEM((16, 16, 208), F32),
            pltpu.VMEM((256, 128), BF),
            pltpu.VMEM((128, 256), BF),
            pltpu.VMEM((128, 896), F32),
            pltpu.VMEM((16, 16, 512), BF),
            pltpu.VMEM((16, 16, 384), BF),
            pltpu.VMEM((16, 16, 512), BF),
            pltpu.VMEM((16, 16, 384), BF),
            pltpu.VMEM((16, 16, 1280), BF),
            pltpu.VMEM((2, 16, 16, 384), BF),
            pltpu.VMEM((2, 16, 16, 384), BF),
            pltpu.VMEM((2, 128, 384), BF),
            pltpu.VMEM((2, 128, 384), BF),
            pltpu.VMEM((8, 128, 256), F32),
            pltpu.VMEM((8, 128, 256), BF),
            dma((32,)),
            dma((1,)),
            dma((1,)),
            dma((3,)),
            dma((3,)),
            dma((2, 3)),
            dma((2, 3)),
            dma((2, 2, 2)),
            dma((2, 2, 4, 2)),
            dma((2, 2, 2)),
            dma((2, 2, 4, 2)),
            dma((2, 16, 2, 2)),
            dma((2, 16, 2)),
            dma((2, 16, 2)),
            dma((2, 16)),
            dma((2, 16)),
            dma((2, 16)),
            dma((2, 16)),
            dma((2,)),
            dma((2,)),
        ],
        compiler_params=pltpu.CompilerParams(
            collective_id=0, has_side_effects=True, vmem_limit_bytes=63 * 2**20
        ),
        name="talker_flow",
    )(
        hidden, owner, w, gain, wq, wk, wv, cache.reshape(16, 4, 2, 48, 256), fill, noisy, fe, fr,
    )


def solution(mesh):
    placed = (
        P(("segment", "mp", "dp"), None),
        P(("segment", "mp", "dp")),
        P("dp", None),
        P(),
        P(),
        P(),
        P(),
        P(("segment", "mp", "dp"), None, None, None),
        P(("segment", "mp", "dp")),
        P(("segment", "mp", "dp"), None),
        P("mp", None),
        P("mp", None),
    )
    return jax.shard_map(
        shards,
        mesh=mesh,
        in_specs=placed,
        out_specs=P(("segment", "mp", "dp"), None),
        check_vma=False,
    )
```

```python
import jax
import jax.numpy as jnp
from jax import lax
from jax.experimental import pallas as pl
from jax.experimental.pallas import tpu as pltpu
from jax.sharding import PartitionSpec as P

MESH = pl.DeviceIdType.MESH
BF = jnp.bfloat16
F32 = jnp.float32
NEG = -1e30
EXP = 1792


def dot(a, b):
    return jnp.dot(a, b, preferred_element_type=F32)


def dot_t(a, b):
    return lax.dot_general(a, b, (((1,), (1,)), ((), ())), preferred_element_type=F32)


def kernel(
    hid_ref, own_hbm, w_ref, gain_ref, wq_ref, wk_ref, wv_ref, kv_ref, len_hbm, noisy_ref, fe_ref, fr_ref,
    out_ref,
    own_ref, len_ref, hid, hin, pout0, pout1, pin0, pin1, wown, wqkv, kbuf, vbuf, noisy, eb, rb, bias, perm, perm_t, pacc, packed0, packed1, inb0, inb1, qkv, outb, retb, mine, part, hpre, hact,
    lsem, w_send, w_recv, h_send, h_recv, p_send, p_recv, f_send1, f_send2, f_fwd1, f_fwd2, f_recv, fs_send, fs_recv,
    a_send, a_recv, r_send, r_recv, x_send, x_recv,
):
    s = lax.axis_index("segment")
    m = lax.axis_index("mp")
    d = lax.axis_index("dp")
    zl, c = d // 2, d % 2
    z = s * 4 + zl
    y, x = m // 4, m % 4
    sib = (s, m, zl * 2 + (1 - c))

    def zdev(dz):
        zz = (z + dz + 8) % 8
        return (zz // 4, m, (zz % 4) * 2 + c)

    def xydev(dx, dy):
        return (s, ((y + dy + 4) % 4) * 4 + (x + dx + 4) % 4, d)

    def rcopy(src, dst, ss, rs, dev):
        return pltpu.make_async_remote_copy(
            src_ref=src, dst_ref=dst, send_sem=ss, recv_sem=rs, device_id=dev, device_id_type=MESH
        )

    barrier = pltpu.get_barrier_semaphore()

    def greet(k, _):
        pl.semaphore_signal(barrier, inc=1, device_id=(s, (m + k) % 16, d), device_id_type=MESH)
        return 0

    for dev in (zdev(1), zdev(-1), zdev(2), zdev(-2), zdev(4), sib):
        pl.semaphore_signal(barrier, inc=1, device_id=dev, device_id_type=MESH)
    lax.fori_loop(1, 16, greet, 0)

    local = []

    def load(src, dst):
        cp = pltpu.make_async_copy(src, dst, lsem.at[len(local)])
        cp.start()
        local.append(cp)
        return cp

    own_s = [load(own_hbm, own_ref), load(len_hbm, len_ref)]
    own_e = []
    for cc in range(2):
        for a in range(2):
            rows = pl.ds(cc * 64 + a * 32, 32)
            own_e.append(load(fe_ref.at[rows], eb.at[m, cc, a]))
            own_e.append(load(fr_ref.at[rows], rb.at[m, cc, a]))
    own_w = load(w_ref, wown.at[c])
    own_h = load(hid_ref.at[:, pl.ds(pl.multiple_of(zl * 896, 128), 896)], hid)
    pl.semaphore_wait(barrier, 21)

    sends = []

    def go(cp):
        cp.start()
        sends.append(cp)

    two = 2 - 4 * c
    steps = (1, -1, two)

    def hcopy(k, dz):
        cols = pl.ds(pl.multiple_of((zl + dz + 4) % 4 * 896, 128), 896)
        return rcopy(hid_ref.at[:, cols], hin.at[k], h_send.at[k], h_recv.at[k], zdev(dz))

    halves = ((pout0, pin0, packed0, inb0, slice(0, 512)), (pout1, pin1, packed1, inb1, slice(512, 896)))

    def pcopy(n, k, dz):
        return rcopy(halves[n][0].at[k], halves[n][1].at[k], p_send.at[n, k], p_recv.at[n, k], zdev(-dz))

    def own_weight(cc):
        return rcopy(w_ref, wown.at[cc], w_send.at[0], w_recv.at[0], sib)

    for k, dz in enumerate(steps):
        go(hcopy(k, dz))
    go(own_weight(c))

    def pid(a, i, j):
        return j * 4 + i if a == 0 else i * 4 + j

    def nb1(a, k):
        return xydev(k, 0) if a == 0 else xydev(0, k)

    def nb2(a, k):
        return xydev(0, k) if a == 0 else xydev(k, 0)

    def at(a):
        return (x, y) if a == 0 else (y, x)

    class Gather:
        def __init__(self, n, buf):
            self.n, self.buf = n, buf

        def full(self, p, a, ss, rs, dev):
            return rcopy(self.buf.at[p, c, a], self.buf.at[p, c, a], ss, rs, dev)

        def piece(self, p, a, k, ss, dev):
            ref = self.buf.at[p, c, a, pl.ds(k * 16, 16)]
            return rcopy(ref, ref, ss, f_recv.at[self.n, p, a, k], dev)

        def got(self, p, a):
            self.full(p, a, f_send1.at[self.n, 0, 0], f_recv.at[self.n, p, a, 0], sib).wait_recv()

        def got_pieces(self, p, a):
            for k in range(2):
                self.piece(p, a, k, f_send1.at[self.n, 0, 0], sib).wait_recv()

        def share(self, p, a):
            self.full(p, a, fs_send.at[self.n, p, a], fs_recv.at[self.n, p, a], sib).start()

        def spread(self, a, i, j):
            p = pid(a, i, j)
            for k in range(2):
                sems = f_send2.at[self.n, a, i, k], f_recv.at[self.n, p, a, 0]
                self.full(p, a, *sems, nb2(a, 1 - 2 * k)).start()

        def begin(self):
            for a in range(2):
                p = pid(a, *at(a))
                for k in range(2):
                    sems = f_send1.at[self.n, a, k], f_recv.at[self.n, p, a, 0]
                    go(self.full(p, a, *sems, nb1(a, 1 - 2 * k)))

        def begin2(self):
            for a in range(2):
                self.spread(a, *at(a))

        def first(self):
            for a in range(2):
                i, j = at(a)
                for k in range(2):
                    p = pid(a, (i + (3 if k == 0 else 1)) % 4, j)
                    self.got(p, a)
                    go(self.piece(p, a, k, f_fwd1.at[self.n, a, k], nb1(a, 1 - 2 * k)))

        def first_spread(self):
            for a in range(2):
                i, j = at(a)
                for k in (1, 3):
                    self.spread(a, (i + k) % 4, j)
                    self.share(pid(a, (i + k) % 4, j), a)

        def first_far(self):
            for a in range(2):
                i, j = at(a)
                i2 = (i + 2) % 4
                self.got_pieces(pid(a, i2, j), a)
                self.spread(a, i2, j)
                self.share(pid(a, i2, j), a)

        def second(self, lo, hi):
            def step(t, _):
                for a in range(2):
                    i, j = at(a)
                    it = (i + t) % 4
                    for k in range(2):
                        p = pid(a, it, (j + (3 if k == 0 else 1)) % 4)
                        self.got(p, a)
                        self.piece(p, a, k, f_fwd2.at[self.n, a, it, k], nb2(a, 1 - 2 * k)).start()
                        self.share(p, a)
                return 0

            lax.fori_loop(lo, hi, step, 0)

        def second_far(self):
            def step(t, _):
                for a in range(2):
                    i, j = at(a)
                    p = pid(a, (i + t) % 4, (j + 2) % 4)
                    self.got_pieces(p, a)
                    self.share(p, a)
                return 0

            lax.fori_loop(0, 4, step, 0)

        def shared(self):
            def step(t, _):
                p = (m + t) % 16
                for a in range(2):
                    dst = self.buf.at[p, 1 - c, a]
                    rcopy(dst, dst, fs_send.at[self.n, p, a], fs_recv.at[self.n, p, a], sib).wait_recv()
                return 0

            lax.fori_loop(1, 16, step, 0)

        def sent(self):
            def step(i, _):
                for a in range(2):
                    p = pid(a, i, at(a)[1])
                    for k in range(2):
                        self.full(p, a, f_send2.at[self.n, a, i, k], f_recv.at[self.n, p, a, 0], sib).wait_send()
                        self.piece(p, a, k, f_fwd2.at[self.n, a, i, k], sib).wait_send()
                return 0

            lax.fori_loop(0, 4, step, 0)

            def step2(t, _):
                p = (m + t) % 16
                for a in range(2):
                    self.full(p, a, fs_send.at[self.n, p, a], fs_recv.at[self.n, p, a], sib).wait_send()
                return 0

            lax.fori_loop(1, 16, step2, 0)

    expand, reduce = Gather(0, eb), Gather(1, rb)
    for cp in own_e:
        cp.wait()
    expand.begin()
    expand.begin2()
    expand.first()
    expand.first_spread()
    reduce.begin()
    reduce.begin2()
    own_q = [
        load(wq_ref, wqkv.at[:, pl.ds(0, 768)]),
        load(wk_ref, wqkv.at[:, pl.ds(768, 256)]),
        load(wv_ref, wqkv.at[:, pl.ds(1024, 256)]),
    ]
    own_n = load(noisy_ref, noisy)
    own_kv = []
    for i in range(4):
        own_kv.append(load(kv_ref.at[:, i, 0], kbuf.at[:, pl.ds(i * 48, 48)]))
        own_kv.append(load(kv_ref.at[:, i, 1], vbuf.at[:, pl.ds(i * 48, 48)]))

    own_w.wait()
    own_weight(1 - c).wait_recv()
    wt = wown[...].reshape(896, 896)

    def partial(n, k):
        pout, cols = halves[n][0], halves[n][4]
        pout[k] = dot(hin[k], wt[:, cols]).astype(BF)
        go(pcopy(n, k, steps[k]))

    for k in range(2):
        hcopy(k, steps[k]).wait_recv()
        partial(0, k)
    expand.first_far()
    hcopy(2, steps[2]).wait_recv()
    partial(0, 2)
    for k in range(3):
        partial(1, k)
    own_h.wait()
    pacc[...] = dot(hid[...], wt)

    for cp in own_s:
        cp.wait()
    r0 = lax.broadcasted_iota(jnp.int32, (16, 208), 0)
    j0 = lax.broadcasted_iota(jnp.int32, (16, 208), 1)
    u0 = j0 - 192
    fresh_ok = (j0 >= 192) & (u0 // 4 == r0 // 4) & (u0 % 4 <= r0 % 4)
    slot0 = j0 // 48
    pos0 = j0 % 48
    same = (j0 < 192) & (slot0 == r0 // 4)

    def make_bias(g, _):
        ln = jnp.zeros((16, 208), jnp.int32)
        for i in range(4):
            ln = jnp.where(slot0 == i, len_ref[g * 4 + i], ln)
        ok = fresh_ok | (same & (pos0 < ln))
        bias[g] = jnp.where(ok, 0.0, NEG)
        return 0

    lax.fori_loop(0, 16, make_bias, 0)

    ri = lax.broadcasted_iota(jnp.int32, (128, 128), 0)
    ci = lax.broadcasted_iota(jnp.int32, (128, 128), 1)

    def owners(k, carry):
        a, b = carry
        o = own_ref[k]
        return jnp.where(ri // 4 == k, o, a), jnp.where(ci // 4 == k, o, b)

    zero = jnp.zeros((128, 128), jnp.int32)
    own_rows, own_cols = lax.fori_loop(0, 32, owners, (zero, zero))
    eq = own_rows == own_cols
    rank_row = jnp.sum(jnp.where(eq & (ri // 4 < ci // 4) & (ri % 4 == 0), 1.0, 0.0), axis=0, keepdims=True)
    rank_col = jnp.sum(jnp.where(eq & (ci // 4 < ri // 4) & (ci % 4 == 0), 1.0, 0.0), axis=1, keepdims=True)
    tgt_row = own_cols[0:1, :] * 16 + rank_row.astype(jnp.int32) * 4 + ci[0:1, :] % 4
    tgt_col = own_rows[:, 0:1] * 16 + rank_col.astype(jnp.int32) * 4 + ri[:, 0:1] % 4
    perm[...] = jnp.where(lax.broadcasted_iota(jnp.int32, (256, 128), 0) == tgt_row, 1.0, 0.0).astype(BF)
    perm_t[...] = jnp.where(lax.broadcasted_iota(jnp.int32, (128, 256), 1) == tgt_col, 1.0, 0.0).astype(BF)

    expand.second(0, 4)
    reduce.first()

    for n in range(2):
        _, pin, packed, inb, cols = halves[n]
        for k in range(3):
            pcopy(n, k, steps[k]).wait_recv()
        projected = pacc[:, cols] + pin[0].astype(F32) + pin[1].astype(F32) + pin[2].astype(F32)
        packed[...] = dot(perm[...], projected.astype(BF)).astype(BF).reshape(16, 16, -1)

        def post(k, _):
            o = (m + k) % 16
            rcopy(packed.at[o], inb.at[m], a_send.at[n, o], a_recv.at[n, m], (s, o, d)).start()
            return 0

        lax.fori_loop(1, 16, post, 0)
        inb[m] = packed[m]

    expand.second_far()
    reduce.first_spread()
    reduce.first_far()
    for cp in own_q + own_kv + [own_n]:
        cp.wait()

    gain = gain_ref[...].astype(F32).reshape(1, 896)
    acc, square = 0.0, 0.0
    for n in range(2):
        _, _, packed, inb, cols = halves[n]

        def arrive(k, _):
            o = (m + k) % 16
            rcopy(packed.at[o], inb.at[o], a_send.at[n, o], a_recv.at[n, o], (s, o, d)).wait()
            return 0

        lax.fori_loop(1, 16, arrive, 0)
        rows = inb[...].reshape(256, -1).astype(F32)
        square += jnp.sum(rows * rows, axis=-1, keepdims=True)
        acc += dot((rows * gain[:, cols]).astype(BF), wqkv[cols, :])
    scale = lax.rsqrt(square * (1 / 896) + 1e-06)
    qkv[...] = (acc * scale).astype(BF).reshape(16, 16, 1280)
    kbuf[:, 192:208, :] = qkv[:, :, 768:1024]
    vbuf[:, 192:208, :] = qkv[:, :, 1024:1280]

    factor = 128 ** (-0.5)

    def give(h, g):
        return rcopy(outb.at[h, g], retb.at[h, m], r_send.at[h, g], r_recv.at[h, m], (s, g, d))

    for h in range(2):
        kcols = slice(h * 128, (h + 1) * 128)
        for q4 in range(4):
            group = range(q4 * 4, q4 * 4 + 4)
            sc = []
            for g in group:
                q = [qkv[g, :, (h * 3 + e) * 128 : (h * 3 + e + 1) * 128] for e in range(3)]
                sc.append(dot_t(jnp.concatenate(q, axis=0), kbuf[g, :, kcols]).reshape(3, 16, 208))
            sc = jnp.stack(sc) * factor + bias[q4 * 4 : q4 * 4 + 4][:, None]
            pr = jnp.exp(sc - jnp.max(sc, axis=-1, keepdims=True))
            inv = (1.0 / jnp.sum(pr, axis=-1, keepdims=True)).reshape(4, 48, 1)
            pr = pr.astype(BF).reshape(4, 48, 208)
            for gg, g in enumerate(group):
                o = (dot(pr[gg], vbuf[g, :, kcols]) * inv[gg]).astype(BF)
                for e in range(3):
                    outb[h, g, :, e * 128 : (e + 1) * 128] = o[e * 16 : (e + 1) * 16]

            def give4(g, _):
                @pl.when(g != m)
                def _():
                    give(h, g).start()

                return 0

            lax.fori_loop(q4 * 4, q4 * 4 + 4, give4, 0)
        retb[h, m] = outb[h, m]
    reduce.second(0, 1)
    swaps = []
    for h in range(2):

        def back(k, _):
            o = (m + k) % 16
            rcopy(outb.at[h, o], retb.at[h, o], r_send.at[h, o], r_recv.at[h, o], (s, o, d)).wait()
            return 0

        lax.fori_loop(1, 16, back, 0)
        mine[h] = dot(perm_t[...], retb[h].reshape(256, 384)).astype(BF)
        swaps.append(rcopy(mine.at[h], part.at[h], x_send.at[h], x_recv.at[h], zdev(4)))
        swaps[h].start()
        if h == 0:
            reduce.second(1, 4)

    expand.shared()

    for t in range(8):
        e = eb[2 * t : 2 * t + 2, :, :, :, 0:1024].reshape(256, 1024)
        hpre[t] = dot_t(noisy[...], e)

    reduce.second_far()
    for cp in sends:
        cp.wait_send()
    expand.sent()
    swaps[0].wait()

    for t in range(8):
        e = eb[2 * t : 2 * t + 2, :, :, :, 1024:1408].reshape(256, 384)
        hpre[t] += dot_t(part[0], e)

    reduce.shared()
    reduce.sent()
    swaps[1].wait()

    for t in range(8):
        e = eb[2 * t : 2 * t + 2, :, :, :, 1408:EXP].reshape(256, 384)
        hact[t] = jax.nn.gelu(hpre[t] + dot_t(part[1], e)).astype(BF)

    h = jnp.concatenate([hact[t] for t in range(8)], axis=1)
    for n in range(4):
        cols = slice(n * 256, (n + 1) * 256)
        r = rb[:, :, :, :, cols].reshape(2048, 256)
        out_ref[:, cols] = (noisy[:, cols].astype(F32) + 0.5 * dot(h, r)).astype(BF)


def shards(hidden, owner, w, gain, wq, wk, wv, cache, fill, noisy, fe, fr):
    any_ = pl.BlockSpec(memory_space=pl.ANY)
    vmem = pl.BlockSpec(memory_space=pltpu.VMEM)
    dma = pltpu.SemaphoreType.DMA
    return pl.pallas_call(
        kernel,
        out_shape=jax.ShapeDtypeStruct((128, 1024), BF),
        in_specs=[any_, any_, any_, vmem, any_, any_, any_, any_, any_, any_, any_, any_],
        out_specs=vmem,
        scratch_shapes=[
            pltpu.SMEM((32,), jnp.int32),
            pltpu.SMEM((64,), jnp.int32),
            pltpu.VMEM((128, 896), BF),
            pltpu.VMEM((3, 128, 896), BF),
            pltpu.VMEM((3, 128, 512), BF),
            pltpu.VMEM((3, 128, 384), BF),
            pltpu.VMEM((3, 128, 512), BF),
            pltpu.VMEM((3, 128, 384), BF),
            pltpu.VMEM((2, 448, 896), BF),
            pltpu.VMEM((896, 1280), BF),
            pltpu.VMEM((16, 208, 256), BF),
            pltpu.VMEM((16, 208, 256), BF),
            pltpu.VMEM((128, 1024), BF),
            pltpu.VMEM((16, 2, 2, 32, EXP), BF),
            pltpu.VMEM((16, 2, 2, 32, 1024), BF),
            pltpu.VMEM((16, 16, 208), F32),
            pltpu.VMEM((256, 128), BF),
            pltpu.VMEM((128, 256), BF),
            pltpu.VMEM((128, 896), F32),
            pltpu.VMEM((16, 16, 512), BF),
            pltpu.VMEM((16, 16, 384), BF),
            pltpu.VMEM((16, 16, 512), BF),
            pltpu.VMEM((16, 16, 384), BF),
            pltpu.VMEM((16, 16, 1280), BF),
            pltpu.VMEM((2, 16, 16, 384), BF),
            pltpu.VMEM((2, 16, 16, 384), BF),
            pltpu.VMEM((2, 128, 384), BF),
            pltpu.VMEM((2, 128, 384), BF),
            pltpu.VMEM((8, 128, 256), F32),
            pltpu.VMEM((8, 128, 256), BF),
            dma((32,)),
            dma((1,)),
            dma((1,)),
            dma((3,)),
            dma((3,)),
            dma((2, 3)),
            dma((2, 3)),
            dma((2, 2, 2)),
            dma((2, 2, 4, 2)),
            dma((2, 2, 2)),
            dma((2, 2, 4, 2)),
            dma((2, 16, 2, 2)),
            dma((2, 16, 2)),
            dma((2, 16, 2)),
            dma((2, 16)),
            dma((2, 16)),
            dma((2, 16)),
            dma((2, 16)),
            dma((2,)),
            dma((2,)),
        ],
        compiler_params=pltpu.CompilerParams(
            collective_id=0, has_side_effects=True, vmem_limit_bytes=63 * 2**20
        ),
        name="talker_flow",
    )(
        hidden, owner, w, gain, wq, wk, wv, cache.reshape(16, 4, 2, 48, 256), fill, noisy, fe, fr,
    )


def solution(mesh):
    placed = (
        P(("segment", "mp", "dp"), None),
        P(("segment", "mp", "dp")),
        P("dp", None),
        P(),
        P(),
        P(),
        P(),
        P(("segment", "mp", "dp"), None, None, None),
        P(("segment", "mp", "dp")),
        P(("segment", "mp", "dp"), None),
        P("mp", None),
        P("mp", None),
    )
    return jax.shard_map(
        shards,
        mesh=mesh,
        in_specs=placed,
        out_specs=P(("segment", "mp", "dp"), None),
        check_vma=False,
    )
```

```python
import jax
import jax.numpy as jnp
from jax import lax
from jax.experimental import pallas as pl
from jax.experimental.pallas import tpu as pltpu
from jax.sharding import PartitionSpec as P

MESH = pl.DeviceIdType.MESH
BF = jnp.bfloat16
F32 = jnp.float32
NEG = -1e30
EXP = 1792


def dot(a, b):
    return jnp.dot(a, b, preferred_element_type=F32)


def dot_t(a, b):
    return lax.dot_general(a, b, (((1,), (1,)), ((), ())), preferred_element_type=F32)


def kernel(
    hid_ref, own_hbm, w_ref, gain_ref, wq_ref, wk_ref, wv_ref, kv_ref, len_hbm, noisy_ref, fe_ref, fr_ref,
    out_ref,
    own_ref, len_ref, hid, hin, pout0, pout1, pin0, pin1, wown, wqkv, kbuf, vbuf, noisy, eb, rb, bias, perm, perm_t, pacc, packed0, packed1, inb0, inb1, qkv, outb, retb, mine, part, hpre, hact, obuf,
    lsem, w_send, w_recv, h_send, h_recv, p_send, p_recv, f_send1, f_send2, f_fwd1, f_fwd2, f_recv, fs_send, fs_recv,
    a_send, a_recv, r_send, r_recv, x_send, x_recv, o_sem,
):
    s = lax.axis_index("segment")
    m = lax.axis_index("mp")
    d = lax.axis_index("dp")
    zl, c = d // 2, d % 2
    z = s * 4 + zl
    y, x = m // 4, m % 4
    sib = (s, m, zl * 2 + (1 - c))

    def zdev(dz):
        zz = (z + dz + 8) % 8
        return (zz // 4, m, (zz % 4) * 2 + c)

    def xydev(dx, dy):
        return (s, ((y + dy + 4) % 4) * 4 + (x + dx + 4) % 4, d)

    def rcopy(src, dst, ss, rs, dev):
        return pltpu.make_async_remote_copy(
            src_ref=src, dst_ref=dst, send_sem=ss, recv_sem=rs, device_id=dev, device_id_type=MESH
        )

    barrier = pltpu.get_barrier_semaphore()

    def greet(k, _):
        pl.semaphore_signal(barrier, inc=1, device_id=(s, (m + k) % 16, d), device_id_type=MESH)
        return 0

    for dev in (zdev(1), zdev(-1), zdev(2), zdev(-2), zdev(4), sib):
        pl.semaphore_signal(barrier, inc=1, device_id=dev, device_id_type=MESH)
    lax.fori_loop(1, 16, greet, 0)

    local = []

    def load(src, dst):
        cp = pltpu.make_async_copy(src, dst, lsem.at[len(local)])
        cp.start()
        local.append(cp)
        return cp

    own_s = [load(own_hbm, own_ref), load(len_hbm, len_ref)]
    own_e = []
    for cc in range(2):
        for a in range(2):
            rows = pl.ds(cc * 64 + a * 32, 32)
            own_e.append(load(fe_ref.at[rows], eb.at[m, cc, a]))
            own_e.append(load(fr_ref.at[rows], rb.at[m, cc, a]))
    own_w = load(w_ref, wown.at[c])
    own_h = load(hid_ref.at[:, pl.ds(pl.multiple_of(zl * 896, 128), 896)], hid)
    pl.semaphore_wait(barrier, 21)

    sends = []

    def go(cp):
        cp.start()
        sends.append(cp)

    two = 2 - 4 * c
    steps = (1, -1, two)

    def hcopy(k, dz):
        cols = pl.ds(pl.multiple_of((zl + dz + 4) % 4 * 896, 128), 896)
        return rcopy(hid_ref.at[:, cols], hin.at[k], h_send.at[k], h_recv.at[k], zdev(dz))

    halves = ((pout0, pin0, packed0, inb0, slice(0, 512)), (pout1, pin1, packed1, inb1, slice(512, 896)))

    def pcopy(n, k, dz):
        return rcopy(halves[n][0].at[k], halves[n][1].at[k], p_send.at[n, k], p_recv.at[n, k], zdev(-dz))

    def own_weight(cc):
        return rcopy(w_ref, wown.at[cc], w_send.at[0], w_recv.at[0], sib)

    for k, dz in enumerate(steps):
        go(hcopy(k, dz))
    go(own_weight(c))

    def pid(a, i, j):
        return j * 4 + i if a == 0 else i * 4 + j

    def nb1(a, k):
        return xydev(k, 0) if a == 0 else xydev(0, k)

    def nb2(a, k):
        return xydev(0, k) if a == 0 else xydev(k, 0)

    def at(a):
        return (x, y) if a == 0 else (y, x)

    class Gather:
        def __init__(self, n, buf):
            self.n, self.buf = n, buf

        def full(self, p, a, ss, rs, dev):
            return rcopy(self.buf.at[p, c, a], self.buf.at[p, c, a], ss, rs, dev)

        def piece(self, p, a, k, ss, dev):
            ref = self.buf.at[p, c, a, pl.ds(k * 16, 16)]
            return rcopy(ref, ref, ss, f_recv.at[self.n, p, a, k], dev)

        def got(self, p, a):
            self.full(p, a, f_send1.at[self.n, 0, 0], f_recv.at[self.n, p, a, 0], sib).wait_recv()

        def got_pieces(self, p, a):
            for k in range(2):
                self.piece(p, a, k, f_send1.at[self.n, 0, 0], sib).wait_recv()

        def share(self, p, a):
            self.full(p, a, fs_send.at[self.n, p, a], fs_recv.at[self.n, p, a], sib).start()

        def spread(self, a, i, j):
            p = pid(a, i, j)
            for k in range(2):
                sems = f_send2.at[self.n, a, i, k], f_recv.at[self.n, p, a, 0]
                self.full(p, a, *sems, nb2(a, 1 - 2 * k)).start()

        def begin(self):
            for a in range(2):
                p = pid(a, *at(a))
                for k in range(2):
                    sems = f_send1.at[self.n, a, k], f_recv.at[self.n, p, a, 0]
                    go(self.full(p, a, *sems, nb1(a, 1 - 2 * k)))

        def begin2(self):
            for a in range(2):
                self.spread(a, *at(a))

        def first(self):
            for a in range(2):
                i, j = at(a)
                for k in range(2):
                    p = pid(a, (i + (3 if k == 0 else 1)) % 4, j)
                    self.got(p, a)
                    go(self.piece(p, a, k, f_fwd1.at[self.n, a, k], nb1(a, 1 - 2 * k)))

        def first_spread(self):
            for a in range(2):
                i, j = at(a)
                for k in (1, 3):
                    self.spread(a, (i + k) % 4, j)
                    self.share(pid(a, (i + k) % 4, j), a)

        def first_far(self):
            for a in range(2):
                i, j = at(a)
                i2 = (i + 2) % 4
                self.got_pieces(pid(a, i2, j), a)
                self.spread(a, i2, j)
                self.share(pid(a, i2, j), a)

        def second(self, lo, hi):
            def step(t, _):
                for a in range(2):
                    i, j = at(a)
                    it = (i + t) % 4
                    for k in range(2):
                        p = pid(a, it, (j + (3 if k == 0 else 1)) % 4)
                        self.got(p, a)
                        self.piece(p, a, k, f_fwd2.at[self.n, a, it, k], nb2(a, 1 - 2 * k)).start()
                        self.share(p, a)
                return 0

            lax.fori_loop(lo, hi, step, 0)

        def second_far(self):
            def step(t, _):
                for a in range(2):
                    i, j = at(a)
                    p = pid(a, (i + t) % 4, (j + 2) % 4)
                    self.got_pieces(p, a)
                    self.share(p, a)
                return 0

            lax.fori_loop(0, 4, step, 0)

        def shared(self):
            def step(t, _):
                p = (m + t) % 16
                for a in range(2):
                    dst = self.buf.at[p, 1 - c, a]
                    rcopy(dst, dst, fs_send.at[self.n, p, a], fs_recv.at[self.n, p, a], sib).wait_recv()
                return 0

            lax.fori_loop(1, 16, step, 0)

        def sent(self):
            def step(i, _):
                for a in range(2):
                    p = pid(a, i, at(a)[1])
                    for k in range(2):
                        self.full(p, a, f_send2.at[self.n, a, i, k], f_recv.at[self.n, p, a, 0], sib).wait_send()
                        self.piece(p, a, k, f_fwd2.at[self.n, a, i, k], sib).wait_send()
                return 0

            lax.fori_loop(0, 4, step, 0)

            def step2(t, _):
                p = (m + t) % 16
                for a in range(2):
                    self.full(p, a, fs_send.at[self.n, p, a], fs_recv.at[self.n, p, a], sib).wait_send()
                return 0

            lax.fori_loop(1, 16, step2, 0)

    expand, reduce = Gather(0, eb), Gather(1, rb)
    for cp in own_e:
        cp.wait()
    expand.begin()
    expand.begin2()
    expand.first()
    expand.first_spread()
    reduce.begin()
    reduce.begin2()
    own_q = [
        load(wq_ref, wqkv.at[:, pl.ds(0, 768)]),
        load(wk_ref, wqkv.at[:, pl.ds(768, 256)]),
        load(wv_ref, wqkv.at[:, pl.ds(1024, 256)]),
    ]
    own_n = load(noisy_ref, noisy)
    own_kv = []
    for i in range(4):
        own_kv.append(load(kv_ref.at[:, i, 0], kbuf.at[:, pl.ds(i * 48, 48)]))
        own_kv.append(load(kv_ref.at[:, i, 1], vbuf.at[:, pl.ds(i * 48, 48)]))

    own_w.wait()
    own_weight(1 - c).wait_recv()
    wt = wown[...].reshape(896, 896)

    def partial(n, k):
        pout, cols = halves[n][0], halves[n][4]
        pout[k] = dot(hin[k], wt[:, cols]).astype(BF)
        go(pcopy(n, k, steps[k]))

    for k in range(2):
        hcopy(k, steps[k]).wait_recv()
        partial(0, k)
    expand.first_far()
    hcopy(2, steps[2]).wait_recv()
    partial(0, 2)
    for k in range(3):
        partial(1, k)
    own_h.wait()
    pacc[...] = dot(hid[...], wt)

    for cp in own_s:
        cp.wait()
    r0 = lax.broadcasted_iota(jnp.int32, (16, 208), 0)
    j0 = lax.broadcasted_iota(jnp.int32, (16, 208), 1)
    u0 = j0 - 192
    fresh_ok = (j0 >= 192) & (u0 // 4 == r0 // 4) & (u0 % 4 <= r0 % 4)
    slot0 = j0 // 48
    pos0 = j0 % 48
    same = (j0 < 192) & (slot0 == r0 // 4)

    def make_bias(g, _):
        ln = jnp.zeros((16, 208), jnp.int32)
        for i in range(4):
            ln = jnp.where(slot0 == i, len_ref[g * 4 + i], ln)
        ok = fresh_ok | (same & (pos0 < ln))
        bias[g] = jnp.where(ok, 0.0, NEG)
        return 0

    lax.fori_loop(0, 16, make_bias, 0)

    ri = lax.broadcasted_iota(jnp.int32, (128, 128), 0)
    ci = lax.broadcasted_iota(jnp.int32, (128, 128), 1)

    def owners(k, carry):
        a, b = carry
        o = own_ref[k]
        return jnp.where(ri // 4 == k, o, a), jnp.where(ci // 4 == k, o, b)

    zero = jnp.zeros((128, 128), jnp.int32)
    own_rows, own_cols = lax.fori_loop(0, 32, owners, (zero, zero))
    eq = own_rows == own_cols
    rank_row = jnp.sum(jnp.where(eq & (ri // 4 < ci // 4) & (ri % 4 == 0), 1.0, 0.0), axis=0, keepdims=True)
    rank_col = jnp.sum(jnp.where(eq & (ci // 4 < ri // 4) & (ci % 4 == 0), 1.0, 0.0), axis=1, keepdims=True)
    tgt_row = own_cols[0:1, :] * 16 + rank_row.astype(jnp.int32) * 4 + ci[0:1, :] % 4
    tgt_col = own_rows[:, 0:1] * 16 + rank_col.astype(jnp.int32) * 4 + ri[:, 0:1] % 4
    perm[...] = jnp.where(lax.broadcasted_iota(jnp.int32, (256, 128), 0) == tgt_row, 1.0, 0.0).astype(BF)
    perm_t[...] = jnp.where(lax.broadcasted_iota(jnp.int32, (128, 256), 1) == tgt_col, 1.0, 0.0).astype(BF)

    expand.second(0, 4)
    reduce.first()

    for n in range(2):
        _, pin, packed, inb, cols = halves[n]
        for k in range(3):
            pcopy(n, k, steps[k]).wait_recv()
        projected = pacc[:, cols] + pin[0].astype(F32) + pin[1].astype(F32) + pin[2].astype(F32)
        packed[...] = dot(perm[...], projected.astype(BF)).astype(BF).reshape(16, 16, -1)

        def post(k, _):
            o = (m + k) % 16
            rcopy(packed.at[o], inb.at[m], a_send.at[n, o], a_recv.at[n, m], (s, o, d)).start()
            return 0

        lax.fori_loop(1, 16, post, 0)
        inb[m] = packed[m]

    expand.second_far()
    reduce.first_spread()
    reduce.first_far()
    for cp in own_q + own_kv + [own_n]:
        cp.wait()

    gain = gain_ref[...].astype(F32).reshape(1, 896)
    acc, square = 0.0, 0.0
    for n in range(2):
        _, _, packed, inb, cols = halves[n]

        def arrive(k, _):
            o = (m + k) % 16
            rcopy(packed.at[o], inb.at[o], a_send.at[n, o], a_recv.at[n, o], (s, o, d)).wait()
            return 0

        lax.fori_loop(1, 16, arrive, 0)
        rows = inb[...].reshape(256, -1).astype(F32)
        square += jnp.sum(rows * rows, axis=-1, keepdims=True)
        acc += dot((rows * gain[:, cols]).astype(BF), wqkv[cols, :])
    scale = lax.rsqrt(square * (1 / 896) + 1e-06)
    qkv[...] = (acc * scale).astype(BF).reshape(16, 16, 1280)
    kbuf[:, 192:208, :] = qkv[:, :, 768:1024]
    vbuf[:, 192:208, :] = qkv[:, :, 1024:1280]

    factor = 128 ** (-0.5)

    def give(h, g):
        return rcopy(outb.at[h, g], retb.at[h, m], r_send.at[h, g], r_recv.at[h, m], (s, g, d))

    for h in range(2):
        kcols = slice(h * 128, (h + 1) * 128)
        for q4 in range(4):
            group = range(q4 * 4, q4 * 4 + 4)
            sc = []
            for g in group:
                q = [qkv[g, :, (h * 3 + e) * 128 : (h * 3 + e + 1) * 128] for e in range(3)]
                sc.append(dot_t(jnp.concatenate(q, axis=0), kbuf[g, :, kcols]).reshape(3, 16, 208))
            sc = jnp.stack(sc) * factor + bias[q4 * 4 : q4 * 4 + 4][:, None]
            pr = jnp.exp(sc - jnp.max(sc, axis=-1, keepdims=True))
            inv = (1.0 / jnp.sum(pr, axis=-1, keepdims=True)).reshape(4, 48, 1)
            pr = pr.astype(BF).reshape(4, 48, 208)
            for gg, g in enumerate(group):
                o = (dot(pr[gg], vbuf[g, :, kcols]) * inv[gg]).astype(BF)
                for e in range(3):
                    outb[h, g, :, e * 128 : (e + 1) * 128] = o[e * 16 : (e + 1) * 16]

            def give4(g, _):
                @pl.when(g != m)
                def _():
                    give(h, g).start()

                return 0

            lax.fori_loop(q4 * 4, q4 * 4 + 4, give4, 0)
        retb[h, m] = outb[h, m]
    reduce.second(0, 1)
    swaps = []
    for h in range(2):

        def back(k, _):
            o = (m + k) % 16
            rcopy(outb.at[h, o], retb.at[h, o], r_send.at[h, o], r_recv.at[h, o], (s, o, d)).wait()
            return 0

        lax.fori_loop(1, 16, back, 0)
        mine[h] = dot(perm_t[...], retb[h].reshape(256, 384)).astype(BF)
        swaps.append(rcopy(mine.at[h], part.at[h], x_send.at[h], x_recv.at[h], zdev(4)))
        swaps[h].start()
        if h == 0:
            reduce.second(1, 4)

    expand.shared()

    for t in range(8):
        e = eb[2 * t : 2 * t + 2, :, :, :, 0:1024].reshape(256, 1024)
        hpre[t] = dot_t(noisy[...], e)

    reduce.second_far()
    for cp in sends:
        cp.wait_send()
    expand.sent()
    swaps[0].wait()

    for t in range(8):
        e = eb[2 * t : 2 * t + 2, :, :, :, 1024:1408].reshape(256, 384)
        hpre[t] += dot_t(part[0], e)

    reduce.shared()
    reduce.sent()
    swaps[1].wait()

    for t in range(8):
        e = eb[2 * t : 2 * t + 2, :, :, :, 1408:EXP].reshape(256, 384)
        hact[t] = jax.nn.gelu(hpre[t] + dot_t(part[1], e)).astype(BF)

    h = jnp.concatenate([hact[t] for t in range(8)], axis=1)
    outs = []
    for n in range(4):
        cols = slice(n * 256, (n + 1) * 256)
        r = rb[:, :, :, :, cols].reshape(2048, 256)
        obuf[:, cols] = (noisy[:, cols].astype(F32) + 0.5 * dot(h, r)).astype(BF)
        done = pltpu.make_async_copy(obuf.at[:, pl.ds(n * 256, 256)], out_ref.at[:, pl.ds(n * 256, 256)], o_sem.at[n])
        done.start()
        outs.append(done)
    for done in outs:
        done.wait()


def shards(hidden, owner, w, gain, wq, wk, wv, cache, fill, noisy, fe, fr):
    any_ = pl.BlockSpec(memory_space=pl.ANY)
    vmem = pl.BlockSpec(memory_space=pltpu.VMEM)
    dma = pltpu.SemaphoreType.DMA
    return pl.pallas_call(
        kernel,
        out_shape=jax.ShapeDtypeStruct((128, 1024), BF),
        in_specs=[any_, any_, any_, vmem, any_, any_, any_, any_, any_, any_, any_, any_],
        out_specs=any_,
        scratch_shapes=[
            pltpu.SMEM((32,), jnp.int32),
            pltpu.SMEM((64,), jnp.int32),
            pltpu.VMEM((128, 896), BF),
            pltpu.VMEM((3, 128, 896), BF),
            pltpu.VMEM((3, 128, 512), BF),
            pltpu.VMEM((3, 128, 384), BF),
            pltpu.VMEM((3, 128, 512), BF),
            pltpu.VMEM((3, 128, 384), BF),
            pltpu.VMEM((2, 448, 896), BF),
            pltpu.VMEM((896, 1280), BF),
            pltpu.VMEM((16, 208, 256), BF),
            pltpu.VMEM((16, 208, 256), BF),
            pltpu.VMEM((128, 1024), BF),
            pltpu.VMEM((16, 2, 2, 32, EXP), BF),
            pltpu.VMEM((16, 2, 2, 32, 1024), BF),
            pltpu.VMEM((16, 16, 208), F32),
            pltpu.VMEM((256, 128), BF),
            pltpu.VMEM((128, 256), BF),
            pltpu.VMEM((128, 896), F32),
            pltpu.VMEM((16, 16, 512), BF),
            pltpu.VMEM((16, 16, 384), BF),
            pltpu.VMEM((16, 16, 512), BF),
            pltpu.VMEM((16, 16, 384), BF),
            pltpu.VMEM((16, 16, 1280), BF),
            pltpu.VMEM((2, 16, 16, 384), BF),
            pltpu.VMEM((2, 16, 16, 384), BF),
            pltpu.VMEM((2, 128, 384), BF),
            pltpu.VMEM((2, 128, 384), BF),
            pltpu.VMEM((8, 128, 256), F32),
            pltpu.VMEM((8, 128, 256), BF),
            pltpu.VMEM((128, 1024), BF),
            dma((32,)),
            dma((1,)),
            dma((1,)),
            dma((3,)),
            dma((3,)),
            dma((2, 3)),
            dma((2, 3)),
            dma((2, 2, 2)),
            dma((2, 2, 4, 2)),
            dma((2, 2, 2)),
            dma((2, 2, 4, 2)),
            dma((2, 16, 2, 2)),
            dma((2, 16, 2)),
            dma((2, 16, 2)),
            dma((2, 16)),
            dma((2, 16)),
            dma((2, 16)),
            dma((2, 16)),
            dma((2,)),
            dma((2,)),
            dma((4,)),
        ],
        compiler_params=pltpu.CompilerParams(
            collective_id=0, has_side_effects=True, vmem_limit_bytes=63 * 2**20
        ),
        name="talker_flow",
    )(
        hidden, owner, w, gain, wq, wk, wv, cache.reshape(16, 4, 2, 48, 256), fill, noisy, fe, fr,
    )


def solution(mesh):
    placed = (
        P(("segment", "mp", "dp"), None),
        P(("segment", "mp", "dp")),
        P("dp", None),
        P(),
        P(),
        P(),
        P(),
        P(("segment", "mp", "dp"), None, None, None),
        P(("segment", "mp", "dp")),
        P(("segment", "mp", "dp"), None),
        P("mp", None),
        P("mp", None),
    )
    return jax.shard_map(
        shards,
        mesh=mesh,
        in_specs=placed,
        out_specs=P(("segment", "mp", "dp"), None),
        check_vma=False,
    )
```
